32 devices in a mesh: cls: 4 (over y, x), rows: 8 (over z, core).
Axes of the slice: x: 2, y: 2, z: 4, core: 2. Of those that a mesh axis runs over, the one named last changes fastest.
Arguments:
- prior: bfloat16 [16384, 1000], P('rows', 'cls'), may hold values from -6 to 6
- blocks: bfloat16 [64, 24, 256, 256], P('rows'), may hold values from -0.078125 to 0.078125
- links: int32 [64, 24], P('rows'), may hold values from 0 to 15, as said below
- counts: int32 [64], P('rows'), may hold values from 1 to 24
- fetch: int32 [8, 8, 1], P('rows'), may hold values from 0 to 7
- seeds: int32 [16384], P('rows'), may hold values from -1000 to 999
- inv_temp: float32 [16384], P('rows'), may hold values from 1 to 300
Outputs:
- pseudo: bfloat16 [16384, 1000], P('rows', 'cls')
- certainty: float32 [16384], P('rows')
The draws below stay inside these ranges and needn't reach their ends.
Inputs may be any that keep to these rules, and one draw needn't show every extreme that they name: links index a slot list of 8 own tiles followed by one tile from each index of rows in order; every one of these slots is named by some link of its index of rows. `seeds`: a negative seed marks an image without a label.
All inputs are finite; a program needn't handle non-finite values.
Results may differ from the reference program's by a relative error of at most 0.0075.
The reference program's roundings to bfloat16 on the way (of `first`) count: a program that leaves them out, or rounds other values in their place, can miss the bound.
Values may be sent and summed in bfloat16 or wider, within the bound.
No kernel may reach another device: no remote copies, remote signals or barrier semaphores. Data moves between devices by JAX's collectives and lax.ppermute only.
A program may use at most 192 MiB of HBM per device.

```python
import math
import jax
import jax.numpy as jnp
from jax import lax

TILE = 256
CLS = 1000
NB = 24
TPD = 8
CAP = 1
TILES = 64
ROWS = 16384
N_ROWS = 8


def draw_links(key, part):
    slot_total = TPD + N_ROWS * CAP

    def per_device(subkey):
        key_extra, key_order = jax.random.split(subkey)
        extra = jax.random.randint(key_extra, (TPD * NB - slot_total,), 0, slot_total, dtype=jnp.int32)
        position_entries = jnp.concatenate([jnp.arange(slot_total, dtype=jnp.int32), extra])
        return jax.random.permutation(key_order, position_entries)
    return jax.vmap(per_device)(jax.random.split(key, N_ROWS)).reshape(TPD * N_ROWS, NB)


def draw_counts(key, part):
    values = jax.random.randint(key, (TPD * N_ROWS,), 1, NB + 1, dtype=jnp.int32)
    return values.at[0].set(NB).at[1].set(1)


def draw_fetch(key, part):
    scores = jax.random.randint(key, (N_ROWS, N_ROWS, TPD), 0, 1 << 20, dtype=jnp.int32)
    scores = scores * TPD + jnp.arange(TPD, dtype=jnp.int32)
    order = jnp.argsort(scores, axis=-1, stable=True).astype(jnp.int32)
    selected_entries = order[..., :CAP]
    return selected_entries.at[0, 0, 0].set(TPD - 1).at[0, 1, 0].set(0)


def draw_inv_temp(key, part):
    key_base = jax.random.fold_in(key, 0)
    base = jnp.exp(jax.random.uniform(key_base, (ROWS,), jnp.float32, 0.0, math.log(8.0)))
    return base


def place_ends(entries, rng, low, largest):
    spot = [jax.random.randint(jax.random.fold_in(rng, axis), (), 0, length) for axis, length in enumerate(entries.shape)]
    widest = entries.shape.index(max(entries.shape))
    neighbour = spot[:widest] + [(spot[widest] + 1) % entries.shape[widest]] + spot[widest + 1:]
    return entries.at[tuple(spot)].set(low).at[tuple(neighbour)].set(largest)


def level_of(rng, shape, shards, least, high):
    def one(position, shards_of):
        heights = jax.random.uniform(jax.random.fold_in(jax.random.fold_in(rng, 6), position), (shards_of,), jnp.float32, least / len(shards), high / len(shards))
        return jnp.repeat(jnp.exp(heights), shape[position] // shards_of).reshape((-1,) + (1,) * (len(shape) - position - 1))

    factor_of = one(*shards[0])
    for cut in shards[1:]:
        factor_of = factor_of * one(*cut)
    return factor_of


def centred(own_key, dims, width, reach, cuts=(), held_as=jnp.bfloat16):
    level = level_of(own_key, dims, cuts, -0.22, 0.18) if cuts else 1.0
    values = jax.random.normal(own_key, dims, jnp.float32) * width * level
    return jnp.minimum(jnp.maximum(values, -reach), reach).astype(held_as)


def setup_inputs(seed: int = 0) -> dict:
    splits = jax.random.split(jax.random.key(seed), 8)
    return {
        "prior": centred(splits[0], (ROWS, CLS), 1.0, 6.0, ((0, 8), (1, 4))),
        "blocks": centred(splits[1], (TILES, NB, TILE, TILE), (NB * TILE) ** -0.5, 0.078125, ((0, 8),)),
        "links": draw_links(jax.random.fold_in(splits[7], 71), 0),
        "counts": draw_counts(jax.random.fold_in(splits[7], 71), 0),
        "fetch": draw_fetch(jax.random.fold_in(splits[7], 71), 0),
        "seeds": place_ends(jax.random.randint(splits[5], (ROWS,), -CLS, CLS), jax.random.fold_in(splits[5], 1), -CLS, CLS - 1).astype(jnp.int32),
        "inv_temp": draw_inv_temp(jax.random.fold_in(splits[7], 71), 0),
    }


blend = 0.8


def column_block_list(links, fetch):
    owner = (jnp.arange(links.shape[0], dtype=jnp.int32) // TPD)[:, None]
    remote = jnp.maximum(links - TPD, 0)
    source = remote // CAP
    place = remote % CAP
    fetched = fetch[owner, source, place]
    return jnp.where(links < TPD, owner * TPD + links, source * TPD + fetched).astype(jnp.int32)


def propagate(field, blocks, tiles_used, live_slots, targets):
    tiled = field.reshape(TILES, TILE, CLS)

    def one_tile(tile_no):
        adjacent_blocks = tiled[tiles_used[tile_no]].astype(jnp.float32)
        adjacent_blocks = jnp.where(live_slots[tile_no][:, None, None], adjacent_blocks, jnp.float32(0.0))
        return jnp.einsum("jab,jbc->ac", blocks[tile_no].astype(jnp.float32), adjacent_blocks)

    accumulated_sum = lax.map(one_tile, jnp.arange(TILES, dtype=jnp.int32))
    return blend * accumulated_sum.reshape(ROWS, CLS) + (1.0 - blend) * targets


def reference(prior, blocks, links, counts, fetch, seeds, inv_temp):
    tiles_used = column_block_list(links, fetch)
    live_slots = jnp.arange(NB, dtype=jnp.int32)[None, :] < counts[:, None]
    targets = (seeds[:, None] == jnp.arange(CLS, dtype=jnp.int32)[None, :]).astype(jnp.float32)
    first = propagate(prior, blocks, tiles_used, live_slots, targets).astype(jnp.bfloat16)
    second = propagate(first, blocks, tiles_used, live_slots, targets)
    logits = inv_temp[:, None] * second
    top = jnp.max(logits, axis=1, keepdims=True)
    shifted = logits - top
    expo = jnp.exp(shifted)
    totals = jnp.sum(expo, axis=1)
    moments = jnp.sum(expo * shifted, axis=1)
    pseudo = (expo / totals[:, None]).astype(jnp.bfloat16)
    certainty = 1.0 - (jnp.log(totals) - moments / totals) / jnp.log(jnp.float32(CLS))
    return pseudo, certainty
```

```python
import functools

import jax
import jax.numpy as jnp
from jax import lax
from jax.experimental import pallas as pl
from jax.experimental.pallas import tpu as pltpu
from jax.sharding import PartitionSpec as P

CLS = 1000
LANES = 128
blend = 0.8

SMEM = pl.BlockSpec(memory_space=pltpu.SMEM)
VMEM = pl.BlockSpec(memory_space=pltpu.VMEM)
ANY = pl.BlockSpec(memory_space=pl.ANY)


def params(mib):
    return pltpu.CompilerParams(vmem_limit_bytes=mib << 20)


def sds(shape, dtype):
    return jax.ShapeDtypeStruct(shape, dtype)


def group_of(slots):
    return next(g for g in (4, 3, 2, 1) if slots % g == 0)


def split_kernel(prior_ref, *outs):
    width = prior_ref.shape[-1]
    for c, out in enumerate(outs):
        start = c * LANES
        live = min(LANES, width - start)
        out[:, :, :live] = prior_ref[:, :, start : start + live]
        if live < LANES:
            out[:, :, live:] = jnp.zeros(out.shape[:2] + (LANES - live,), out.dtype)


def split(prior, tile_rows):
    tiles = prior.reshape(-1, tile_rows, prior.shape[1])
    chunks = pl.cdiv(prior.shape[1], LANES)
    shape = sds((tiles.shape[0], tile_rows, LANES), prior.dtype)
    return pl.pallas_call(
        split_kernel,
        out_shape=[shape] * chunks,
        in_specs=[VMEM],
        out_specs=[VMEM] * chunks,
        compiler_params=params(16),
        name="split",
    )(tiles)


def pick_kernel(chunks, me_ref, wanted_ref, *refs):
    tabs, outs, sems = refs[:chunks], refs[chunks : 3 * chunks], refs[-1]
    n = wanted_ref.shape[0]
    copies = []
    for c in range(chunks):
        for x in range(n):
            tile = wanted_ref[me_ref[0] ^ x]
            copies.append(
                pltpu.make_async_copy(tabs[c].at[tile], outs[2 * c + x % 2].at[x // 2], sems.at[c, x])
            )
            copies[-1].start()
    for copy in copies:
        copy.wait()


def pick(me, wanted, tabs):
    n = wanted.shape[0]
    chunks = len(tabs)
    shape = sds((n // 2,) + tabs[0].shape[1:], tabs[0].dtype)
    outs = pl.pallas_call(
        functools.partial(pick_kernel, chunks),
        out_shape=[shape] * (2 * chunks),
        in_specs=[SMEM, SMEM] + [ANY] * chunks,
        out_specs=[ANY] * (2 * chunks),
        scratch_shapes=[pltpu.SemaphoreType.DMA((chunks, n))],
        compiler_params=params(16),
        name="pick",
    )(me, wanted, *tabs)
    return [outs[2 * c : 2 * c + 2] for c in range(chunks)]


def exchange(straight, across, n):
    got = lax.ppermute(across, "rows", [(i, i ^ 1) for i in range(n)])
    arrived = []
    for k in range(n // 2 - 1, 0, -1):
        message = jnp.stack([straight[k], got[k]])
        arrived.append(lax.ppermute(message, "rows", [(i, i ^ (2 * k)) for i in range(n)]))
    return got, arrived[::-1]


def load_field(tab, got, arrived, field, sems):
    own = tab.shape[0]
    copies = [pltpu.make_async_copy(tab, field.at[pl.ds(0, own)], sems.at[0])]
    copies.append(pltpu.make_async_copy(got.at[0], field.at[own + 1], sems.at[1]))
    for k, one in enumerate(arrived):
        copies.append(
            pltpu.make_async_copy(one, field.at[pl.ds(own + 2 * (k + 1), 2)], sems.at[2 + k])
        )
    for copy in copies:
        copy.start()
    field[own] = jnp.zeros(field.shape[1:], field.dtype)
    return copies


def block_copy(blocks, held, sems, t, g):
    size = held.shape[1] // sems.shape[1]
    span = pl.ds(g * size, size)
    return pltpu.make_async_copy(blocks.at[t, span], held.at[t, span], sems.at[t, g])


def start_blocks(groups_of, blocks, held, sems):
    for t in range(held.shape[0]):
        groups = groups_of(t)
        for g in range(sems.shape[1]):

            @pl.when(g < groups)
            def _():
                block_copy(blocks, held, sems, t, g).start()


def tile_sum(t, groups, slots_ref, blocks, held, field, sems):
    slots = held.shape[1]
    size = slots // sems.shape[1]

    def step(g, total):
        block_copy(blocks, held, sems, t, g).wait()
        for i in range(size):
            at = g * size + i
            total = total + jnp.dot(
                held[t, at], field[slots_ref[t * slots + at]], preferred_element_type=jnp.float32
            )
        return total

    return lax.fori_loop(0, groups, step, jnp.zeros(field.shape[1:], jnp.float32))


def with_targets(total, seeds, first_col):
    cols = first_col + lax.broadcasted_iota(jnp.int32, total.shape, 1)
    return blend * total + (1.0 - blend) * (seeds == cols).astype(jnp.float32)


def step1_kernel(
    links, chunk, me_ref, slots_ref, counts_ref, wanted_ref, tab, got, *refs
):
    arrived = refs[:links]
    (blocks, seeds_ref, out, straight, across, field, held, field_sems, sems) = refs[links:]
    own, tile_rows = tab.shape[:2]
    size = held.shape[1] // sems.shape[1]
    groups_of = lambda t: (counts_ref[t] + size - 1) // size
    copies = load_field(tab, got, arrived, field, field_sems)
    start_blocks(groups_of, blocks, held, sems)
    for copy in copies:
        copy.wait()
    first_col = me_ref[1] + chunk * LANES

    def tile(t, carry):
        total = tile_sum(t, groups_of(t), slots_ref, blocks, held, field, sems)
        seeds = seeds_ref[pl.ds(t * tile_rows, tile_rows), :]
        out[t] = with_targets(total, seeds, first_col).astype(out.dtype)
        return carry

    lax.fori_loop(0, own, tile, 0)
    for x in range(wanted_ref.shape[0]):
        (across if x % 2 else straight)[x // 2] = out[wanted_ref[me_ref[0] ^ x]]


def scratch(own, n, tile_rows, dtype, blocks, links):
    slots = blocks.shape[1]
    return [
        pltpu.VMEM((own + n, tile_rows, LANES), dtype),
        pltpu.VMEM(blocks.shape, blocks.dtype),
        pltpu.SemaphoreType.DMA((2 + links,)),
        pltpu.SemaphoreType.DMA((own, slots // group_of(slots))),
    ]


def cost(blocks):
    own, slots, rows, depth = blocks.shape
    return pl.CostEstimate(
        flops=2 * own * slots * rows * depth * LANES,
        bytes_accessed=blocks.size * blocks.dtype.itemsize * 2 // 3,
        transcendentals=0,
    )


def step1(chunk, me, slots, counts, wanted, tab, got, arrived, blocks, seeds):
    own, tile_rows = tab.shape[:2]
    n = wanted.shape[0]
    half = sds((n // 2, tile_rows, LANES), tab.dtype)
    return pl.pallas_call(
        functools.partial(step1_kernel, len(arrived), chunk),
        out_shape=[sds(tab.shape, tab.dtype), half, half],
        in_specs=[SMEM] * 4 + [ANY] * (3 + len(arrived)) + [VMEM],
        out_specs=[VMEM] * 3,
        scratch_shapes=scratch(own, n, tile_rows, tab.dtype, blocks, len(arrived)),
        compiler_params=params(44),
        cost_estimate=cost(blocks),
        name="step1",
    )(me, slots, counts, wanted, tab, got, *arrived, blocks, seeds)


def step2_kernel(links, chunk, width, me_ref, slots_ref, counts_ref, tab, got, *refs):
    arrived = refs[:links]
    (blocks, seeds_ref, temp_ref, expo_ref, stats_ref, field, held, field_sems, sems) = refs[links:]
    own, tile_rows = tab.shape[:2]
    size = held.shape[1] // sems.shape[1]
    groups_of = lambda t: (counts_ref[t] + size - 1) // size
    copies = load_field(tab, got, arrived, field, field_sems)
    start_blocks(groups_of, blocks, held, sems)
    for copy in copies:
        copy.wait()
    first_col = me_ref[1] + chunk * LANES
    live = min(LANES, width - chunk * LANES)

    def tile(t, carry):
        total = tile_sum(t, groups_of(t), slots_ref, blocks, held, field, sems)
        span = pl.ds(pl.multiple_of(t * tile_rows, tile_rows), tile_rows)
        logits = temp_ref[span, :] * with_targets(total, seeds_ref[span, :], first_col)
        lane = lax.broadcasted_iota(jnp.int32, logits.shape, 1)
        if live < LANES:
            top = jnp.max(jnp.where(lane < live, logits, -jnp.inf), axis=1, keepdims=True)
            shifted = jnp.where(lane < live, logits - top, 0.0)
            expo = jnp.where(lane < live, jnp.exp(shifted), 0.0)
        else:
            top = jnp.max(logits, axis=1, keepdims=True)
            shifted = logits - top
            expo = jnp.exp(shifted)
        totals = jnp.sum(expo, axis=1, keepdims=True)
        moments = jnp.sum(expo * shifted, axis=1, keepdims=True)
        expo_ref[span, :] = expo
        summary = jnp.where(lane == 0, top, jnp.where(lane == 1, totals, moments))
        stats_ref[:, span] = summary.T[:8]
        return carry

    lax.fori_loop(0, own, tile, 0)


def step2(chunk, width, me, slots, counts, tab, got, arrived, blocks, seeds, temp):
    own, tile_rows = tab.shape[:2]
    n = 2 * (len(arrived) + 1)
    rows = own * tile_rows
    return pl.pallas_call(
        functools.partial(step2_kernel, len(arrived), chunk, width),
        out_shape=[sds((rows, LANES), jnp.float32), sds((8, rows), jnp.float32)],
        in_specs=[SMEM] * 3 + [ANY] * (3 + len(arrived)) + [VMEM] * 2,
        out_specs=[VMEM] * 2,
        scratch_shapes=scratch(own, n, tile_rows, tab.dtype, blocks, len(arrived)),
        compiler_params=params(44),
        cost_estimate=cost(blocks),
        name="step2",
    )(me, slots, counts, tab, got, *arrived, blocks, seeds, temp)


def finish_kernel(chunks, parts, tile_rows, *refs):
    expos, stats = refs[:chunks], refs[chunks : chunks + chunks * parts]
    pseudo_ref, certainty_ref = refs[chunks + chunks * parts :]
    rows, width = pseudo_ref.shape
    tops = [s[0:1, :] for s in stats]
    top = functools.reduce(jnp.maximum, tops)
    totals = jnp.zeros((1, rows), jnp.float32)
    moments = jnp.zeros((1, rows), jnp.float32)
    scales = []
    for s, one in zip(stats, tops):
        delta = one - top
        scale = jnp.exp(delta)
        scales.append(scale)
        totals += scale * s[1:2, :]
        moments += scale * (s[2:3, :] + delta * s[1:2, :])
    certainty_ref[...] = 1.0 - (jnp.log(totals) - moments / totals) / jnp.log(jnp.float32(CLS))
    inverse = 1.0 / totals
    mine = [scales[c * parts] * inverse for c in range(chunks)]
    mine = jnp.concatenate(mine + [jnp.zeros((LANES - chunks, rows), jnp.float32)], axis=0)
    for t in range(rows // tile_rows):
        span = slice(t * tile_rows, (t + 1) * tile_rows)
        columns = mine[:, span].T
        for c in range(chunks):
            start = c * LANES
            live = min(LANES, width - start)
            value = expos[c][span, :] * columns[:, c : c + 1]
            pseudo_ref[span, start : start + live] = value[:, :live].astype(pseudo_ref.dtype)


def finish(expos, stats, tile_rows, width):
    rows = expos[0].shape[0]
    chunks, parts = len(expos), len(stats[0])
    flat = [s for part in stats for s in part]
    return pl.pallas_call(
        functools.partial(finish_kernel, chunks, parts, tile_rows),
        out_shape=[sds((rows, width), jnp.bfloat16), sds((1, rows), jnp.float32)],
        in_specs=[VMEM] * (len(expos) + len(flat)),
        out_specs=[VMEM] * 2,
        compiler_params=params(24),
        name="finish",
    )(*expos, *flat)


def local(prior, blocks, links, counts, fetch, seeds, inv_temp):
    width = prior.shape[1]
    own, slots, tile_rows = blocks.shape[:3]
    n = lax.axis_size("rows")
    parts = lax.axis_size("cls")
    chunks = pl.cdiv(width, LANES)
    index = lax.axis_index("rows")
    me = jnp.stack([index, lax.axis_index("cls") * width]).astype(jnp.int32)
    wanted = lax.all_to_all(fetch, "rows", split_axis=1, concat_axis=0, tiled=True).reshape(-1)
    tabs = split(prior, tile_rows)

    offset = (links - own) ^ index
    mine = fetch.reshape(n)[index]
    table = jnp.where(links < own, links, jnp.where(offset == 0, mine, own + offset))
    live = jnp.arange(slots, dtype=jnp.int32)[None, :] < counts[:, None]
    table = jnp.where(live, table, own).astype(jnp.int32).reshape(-1)
    seeds = seeds[:, None]
    temp = inv_temp[:, None]

    sent = pick(me, wanted, tabs)
    here = [exchange(*sent[c], n) for c in range(chunks)]
    fields = []
    for c in range(chunks):
        out, straight, across = step1(
            c, me, table, counts, wanted, tabs[c], *here[c], blocks, seeds
        )
        fields.append((out, *exchange(straight, across, n)))
    expos, stats = [], []
    for c in range(chunks):
        expo, summary = step2(c, width, me, table, counts, *fields[c], blocks, seeds, temp)
        expos.append(expo)
        stats.append(
            [summary]
            + [
                lax.ppermute(summary, "cls", [(i, (i + k) % parts) for i in range(parts)])
                for k in range(1, parts)
            ]
        )
    pseudo, certainty = finish(expos, stats, tile_rows, width)
    return pseudo, certainty.reshape(-1)


def solution(mesh):
    return jax.shard_map(
        local,
        mesh=mesh,
        in_specs=(
            P("rows", "cls"),
            P("rows", None, None, None),
            P("rows", None),
            P("rows"),
            P("rows", None, None),
            P("rows"),
            P("rows"),
        ),
        out_specs=(P("rows", "cls"), P("rows")),
        check_vma=False,
    )
```

```python
import functools

import jax
import jax.numpy as jnp
from jax import lax
from jax.experimental import pallas as pl
from jax.experimental.pallas import tpu as pltpu
from jax.sharding import PartitionSpec as P

CLS = 1000
LANES = 128
GROUP = 16
blend = 0.8

SMEM = pl.BlockSpec(memory_space=pltpu.SMEM)
VMEM = pl.BlockSpec(memory_space=pltpu.VMEM)
ANY = pl.BlockSpec(memory_space=pl.ANY)
T_SHIFT, B_SHIFT = 20, 8


def params(mib):
    return pltpu.CompilerParams(vmem_limit_bytes=mib << 20)


def held(shape, dtype):
    return pltpu.VMEM(shape, dtype)


def sds(shape, dtype):
    return jax.ShapeDtypeStruct(shape, dtype)


def split_kernel(prior_ref, *outs):
    width = prior_ref.shape[-1]
    for c, out in enumerate(outs):
        start = c * LANES
        live = min(LANES, width - start)
        out[:, :, :live] = prior_ref[:, :, start : start + live]
        if live < LANES:
            out[:, :, live:] = jnp.zeros(out.shape[:2] + (LANES - live,), out.dtype)


def split(prior, tile_rows):
    tiles = prior.reshape(-1, tile_rows, prior.shape[1])
    chunks = pl.cdiv(prior.shape[1], LANES)
    return pl.pallas_call(
        split_kernel,
        out_shape=[held((tiles.shape[0], tile_rows, LANES), prior.dtype)] * chunks,
        in_specs=[VMEM],
        out_specs=[VMEM] * chunks,
        compiler_params=params(8),
        name="split",
    )(tiles)


def fill_lists(room, index, links_ref, counts_ref, fetch_ref, items_ref, sizes_ref):
    own, slots = links_ref.shape
    n = fetch_ref.shape[1]
    mine = fetch_ref[0, index, 0]

    def tile(t, sizes):
        def slot(j, sizes):
            v = links_ref[t, j]
            x = (v - own) ^ index
            is_own = jnp.logical_or(v < own, x == 0)
            kind = jnp.where(is_own, 0, jnp.where(x < n // 2, 1, 2))
            field = jnp.where(is_own, jnp.where(v < own, v, mine), x)
            place = jnp.where(kind == 0, sizes[0], jnp.where(kind == 1, sizes[1], sizes[2]))
            items_ref[kind * room + place] = (t << T_SHIFT) + ((t * slots + j) << B_SHIFT) + field
            return tuple(s + (kind == i).astype(jnp.int32) for i, s in enumerate(sizes))

        return lax.fori_loop(0, counts_ref[t], slot, sizes)

    sizes = lax.fori_loop(0, own, tile, (jnp.int32(0),) * 3)
    for kind in range(3):
        sizes_ref[kind] = sizes[kind]

        def fill(i, carry):
            items_ref[kind * room + sizes[kind] + i] = own << T_SHIFT
            return carry

        lax.fori_loop(0, GROUP, fill, 0)


def pick_kernel(chunks, me_ref, wanted_ref, *refs):
    tabs, outs = refs[:chunks], refs[chunks:]
    for c in range(chunks):
        for x in range(wanted_ref.shape[0]):
            outs[2 * c + x % 2][x // 2] = tabs[c][wanted_ref[me_ref[0] ^ x, 0, 0]]


def pick(me, wanted, tabs):
    n = wanted.shape[0]
    chunks = len(tabs)
    outs = pl.pallas_call(
        functools.partial(pick_kernel, chunks),
        out_shape=[held((n // 2,) + tabs[0].shape[1:], tabs[0].dtype)] * (2 * chunks),
        in_specs=[SMEM, SMEM] + [VMEM] * chunks,
        out_specs=[VMEM] * (2 * chunks),
        compiler_params=params(8),
        name="pick",
    )(me, wanted, *tabs)
    return [outs[2 * c : 2 * c + 2] for c in range(chunks)]


def after(value, *others):
    return lax.optimization_barrier((value, others))[0]


def across_core(across, n):
    pairs = [(i, i ^ 1) for i in range(n)]
    return [lax.ppermute(across[k], "rows", pairs) for k in range(across.shape[0])]


def messages(straight, got):
    return [jnp.stack([straight[k], got[k]]) for k in range(1, len(got))]


def send(parts, n):
    order = range(len(parts) - 1, -1, -1)
    arrived = [
        lax.ppermute(parts[k], "rows", [(i, i ^ (2 * k + 2)) for i in range(n)]) for k in order
    ]
    return arrived[::-1]


def run_list(kind, items_ref, sizes_ref, room, blocks, rhs, totals, ready=None):
    own = totals[0].shape[0] - 1
    low, high = (1 << B_SHIFT) - 1, (1 << (T_SHIFT - B_SHIFT)) - 1

    def step(g, waited):
        at = kind * room + g * GROUP
        if ready is not None:
            last = jnp.minimum(items_ref[at + GROUP - 1] >> T_SHIFT, own - 1) + 1
            lax.fori_loop(waited, last, ready, 0)
            waited = jnp.maximum(waited, last)
        for i in range(GROUP):
            word = items_ref[at + i]
            t = word >> T_SHIFT
            value = jnp.dot(
                blocks[(word >> B_SHIFT) & high],
                rhs(word & low),
                preferred_element_type=jnp.float32,
            )
            for c, total in enumerate(totals):
                total[t] += value[:, c * LANES : (c + 1) * LANES]
        return waited

    groups = (sizes_ref[kind] + GROUP - 1) // GROUP
    waited = lax.fori_loop(0, groups, step, jnp.int32(0))
    if ready is not None:
        lax.fori_loop(waited, own, ready, 0)


def column(ref, t, tile_rows):
    parts = tile_rows // LANES
    rows = [ref[pl.ds(t * parts + i, 1), :] for i in range(parts)]
    return jnp.concatenate(
        [jnp.broadcast_to(row, (LANES, LANES)).T for row in rows], axis=0
    )


def start_totals(me_ref, seeds_ref, totals):
    own, tile_rows = totals[0].shape[0] - 1, totals[0].shape[1]
    share = (1.0 - blend) / blend
    lane = lax.broadcasted_iota(jnp.int32, totals[0].shape[1:], 1)
    for t in range(own):
        seeds = column(seeds_ref, t, tile_rows) - me_ref[1]
        for c, total in enumerate(totals):
            total[t] = jnp.where(seeds == lane + c * LANES, share, 0.0)


def side_by_side(tabs):
    return lambda f: jnp.concatenate([tab[f] for tab in tabs], axis=1)


def begin_kernel(
    chunks, room, me_ref, links_ref, counts_ref, fetch_ref, blocks_hbm, seeds_ref, temp_ref, *refs
):
    tabs = refs[:chunks]
    items_ref, sizes_ref, blocks, wide_ref = refs[chunks : chunks + 4]
    totals, sems = refs[chunks + 4 : -1], refs[-1]
    own, slots = links_ref.shape
    tile_rows = blocks.shape[1]
    groups = sems.shape[1]
    size = slots // groups

    def copy(t, g):
        return pltpu.make_async_copy(
            blocks_hbm.at[pl.ds(t * slots + g * size, size)],
            blocks.at[pl.ds(t * slots + g * size, size)],
            sems.at[t, g],
        )

    def used(t):
        return (counts_ref[t] + size - 1) // size

    def begin(t, carry):
        return lax.fori_loop(0, used(t), lambda g, c: (copy(t, g).start(), c)[1], carry)

    def ready(t, carry):
        return lax.fori_loop(0, used(t), lambda g, c: (copy(t, g).wait(), c)[1], carry)

    lax.fori_loop(0, own, begin, 0)
    fill_lists(room, me_ref[0], links_ref, counts_ref, fetch_ref, items_ref, sizes_ref)
    for t in range(own):
        wide_ref[t] = blend * column(temp_ref, t, tile_rows)
    start_totals(me_ref, seeds_ref, totals)
    run_list(0, items_ref, sizes_ref, room, blocks, side_by_side(tabs), totals, ready)


def begin(me, links, counts, fetch, blocks, seeds, temp, tabs):
    own, tile_rows = tabs[0].shape[:2]
    slots = links.shape[1]
    room = links.size + GROUP
    chunks = len(tabs)
    size = next(g for g in (4, 3, 2, 1) if slots % g == 0)
    out = pl.pallas_call(
        functools.partial(begin_kernel, chunks, room),
        out_shape=[
            sds((3 * room,), jnp.int32),
            sds((3,), jnp.int32),
            held(blocks.shape, blocks.dtype),
            held(tabs[0].shape, jnp.float32),
        ]
        + [held((own + 1, tile_rows, LANES), jnp.float32)] * chunks,
        in_specs=[SMEM] * 4 + [ANY] + [VMEM] * (2 + chunks),
        out_specs=[SMEM] * 2 + [VMEM] * (2 + chunks),
        scratch_shapes=[pltpu.SemaphoreType.DMA((own, slots // size))],
        compiler_params=params(8),
        cost_estimate=COST,
        name="begin",
    )(me, links, counts, fetch, blocks, seeds, temp, *tabs)
    return out[:2], out[2], out[3], out[4:]


def own_kernel(chunks, room, me_ref, items_ref, sizes_ref, blocks, seeds_ref, *refs):
    tabs, totals = refs[:chunks], refs[chunks:]
    start_totals(me_ref, seeds_ref, totals)
    run_list(0, items_ref, sizes_ref, room, blocks, side_by_side(tabs), totals)


COST = pl.CostEstimate(flops=1, bytes_accessed=1, transcendentals=0)


def own_part(me, items, sizes, blocks, seeds, tabs):
    own, tile_rows = tabs[0].shape[:2]
    chunks = len(tabs)
    return pl.pallas_call(
        functools.partial(own_kernel, chunks, items.shape[0] // 3),
        out_shape=[held((own + 1, tile_rows, LANES), jnp.float32)] * chunks,
        in_specs=[SMEM] * 3 + [VMEM] * (2 + chunks),
        out_specs=[VMEM] * chunks,
        compiler_params=params(8),
        cost_estimate=COST,
        name="own_part",
    )(me, items, sizes, blocks, seeds, *tabs)


def gather_field(kinds, got, arrived, field):
    half = field.shape[0] // 2
    if 1 in kinds:
        field[1] = got[...]
    for k, one in enumerate(arrived):
        x = 2 * (k + 1)
        if (1 if x < half else 2) in kinds:
            field[x] = one[0]
            field[x + 1] = one[1]


def step1_kernel(links, room, me_ref, items_ref, sizes_ref, wanted_ref, blocks, got, *refs):
    arrived = refs[:links]
    begun, out, straight, across, field, total = refs[links:]
    own = out.shape[0]
    gather_field((1, 2), got, arrived, field)
    total[...] = begun[...]
    for kind in (1, 2):
        run_list(kind, items_ref, sizes_ref, room, blocks, lambda f: field[f], [total])
    for t in range(own):
        out[t] = (blend * total[t]).astype(out.dtype)
    for x in range(wanted_ref.shape[0]):
        (across if x % 2 else straight)[x // 2] = out[wanted_ref[me_ref[0] ^ x, 0, 0]]


def step1(me, items, sizes, wanted, blocks, got, arrived, begun):
    own, tile_rows = begun.shape[0] - 1, begun.shape[1]
    n = wanted.shape[0]
    half = held((n // 2, tile_rows, LANES), got.dtype)
    return pl.pallas_call(
        functools.partial(step1_kernel, len(arrived), items.shape[0] // 3),
        out_shape=[held((own, tile_rows, LANES), got.dtype), half, half],
        in_specs=[SMEM] * 4 + [VMEM] * (3 + len(arrived)),
        out_specs=[VMEM] * 3,
        scratch_shapes=[
            pltpu.VMEM((n, tile_rows, LANES), got.dtype),
            pltpu.VMEM(begun.shape, begun.dtype),
        ],
        compiler_params=params(12),
        cost_estimate=COST,
        name="step1",
    )(me, items, sizes, wanted, blocks, got, *arrived, begun)


def near_kernel(links, room, items_ref, sizes_ref, blocks, got, *refs):
    arrived = refs[:links]
    begun, total, field = refs[links:]
    gather_field((1,), got, arrived, field)
    total[...] = begun[...]
    run_list(1, items_ref, sizes_ref, room, blocks, lambda f: field[f], [total])


def near_part(items, sizes, blocks, got, arrived, begun, n):
    tile_rows = begun.shape[1]
    return pl.pallas_call(
        functools.partial(near_kernel, len(arrived), items.shape[0] // 3),
        out_shape=held(begun.shape, begun.dtype),
        in_specs=[SMEM] * 2 + [VMEM] * (3 + len(arrived)),
        out_specs=VMEM,
        scratch_shapes=[pltpu.VMEM((n, tile_rows, LANES), got.dtype)],
        compiler_params=params(8),
        cost_estimate=COST,
        name="near_part",
    )(items, sizes, blocks, got, *arrived, begun)


def step2_kernel(links, live, room, items_ref, sizes_ref, blocks, got, *refs):
    arrived = refs[:links]
    begun, wide_ref, expo_ref, stats_ref, field, total = refs[links:]
    own, tile_rows = expo_ref.shape[:2]
    gather_field((2,), got, arrived, field)
    total[...] = begun[...]
    run_list(2, items_ref, sizes_ref, room, blocks, lambda f: field[f], [total])
    parts = tile_rows // LANES
    for t in range(own):
        logits = wide_ref[t] * total[t]
        lane = lax.broadcasted_iota(jnp.int32, logits.shape, 1)
        if live < LANES:
            top = jnp.max(jnp.where(lane < live, logits, -jnp.inf), axis=1, keepdims=True)
            shifted = jnp.where(lane < live, logits - top, 0.0)
            expo = jnp.where(lane < live, jnp.exp(shifted), 0.0)
        else:
            top = jnp.max(logits, axis=1, keepdims=True)
            shifted = logits - top
            expo = jnp.exp(shifted)
        sums = jnp.sum(expo, axis=1, keepdims=True)
        moments = jnp.sum(expo * shifted, axis=1, keepdims=True)
        expo_ref[t] = expo
        summary = jnp.where(lane == 0, top, jnp.where(lane == 1, sums, moments))
        for i in range(parts):
            flat = summary[i * LANES : (i + 1) * LANES, :].T
            for q in range(3):
                stats_ref[q, t * parts + i : t * parts + i + 1, :] = flat[q : q + 1]


def step2(live, items, sizes, blocks, got, arrived, begun, wide):
    own, tile_rows = begun.shape[0] - 1, begun.shape[1]
    n = 2 * (len(arrived) + 1)
    return pl.pallas_call(
        functools.partial(step2_kernel, len(arrived), live, items.shape[0] // 3),
        out_shape=[
            held((own, tile_rows, LANES), jnp.float32),
            held((3, own * tile_rows // LANES, LANES), jnp.float32),
        ],
        in_specs=[SMEM] * 2 + [VMEM] * (4 + len(arrived)),
        out_specs=[VMEM] * 2,
        scratch_shapes=[
            pltpu.VMEM((n, tile_rows, LANES), got.dtype),
            pltpu.VMEM(begun.shape, begun.dtype),
        ],
        compiler_params=params(12),
        cost_estimate=COST,
        name="step2",
    )(items, sizes, blocks, got, *arrived, begun, wide)


def finish_kernel(chunks, parts, *refs):
    expos, stats = refs[:chunks], refs[chunks : chunks + chunks * parts]
    pseudo_ref, certainty_ref, scale_ref = refs[chunks + chunks * parts :]
    own, tile_rows = expos[0].shape[:2]
    width = pseudo_ref.shape[1]
    top = functools.reduce(jnp.maximum, [s[0] for s in stats])
    totals, moments, scales = 0.0, 0.0, []
    for s in stats:
        delta = s[0] - top
        scale = jnp.exp(delta)
        scales.append(scale)
        totals += scale * s[1]
        moments += scale * (s[2] + delta * s[1])
    certainty_ref[...] = 1.0 - (jnp.log(totals) - moments / totals) / jnp.log(jnp.float32(CLS))
    inverse = 1.0 / totals
    for c in range(chunks):
        scale_ref[c] = scales[c * parts] * inverse
    for t in range(own):
        span = slice(t * tile_rows, (t + 1) * tile_rows)
        for c in range(chunks):
            start = c * LANES
            live = min(LANES, width - start)
            value = expos[c][t] * column(scale_ref.at[c], t, tile_rows)
            pseudo_ref[span, start : start + live] = value[:, :live].astype(pseudo_ref.dtype)


def finish(expos, stats, width):
    own, tile_rows = expos[0].shape[:2]
    rows = own * tile_rows
    chunks, parts = len(expos), len(stats[0])
    flat = [s for part in stats for s in part]
    return pl.pallas_call(
        functools.partial(finish_kernel, chunks, parts),
        out_shape=[sds((rows, width), jnp.bfloat16), sds((rows // LANES, LANES), jnp.float32)],
        in_specs=[VMEM] * (len(expos) + len(flat)),
        out_specs=[VMEM] * 2,
        scratch_shapes=[pltpu.VMEM((chunks, rows // LANES, LANES), jnp.float32)],
        compiler_params=params(12),
        name="finish",
    )(*expos, *flat)


def local(prior, blocks, links, counts, fetch, seeds, inv_temp):
    width = prior.shape[1]
    tile_rows = blocks.shape[2]
    n = lax.axis_size("rows")
    parts = lax.axis_size("cls")
    chunks = pl.cdiv(width, LANES)
    me = jnp.stack([lax.axis_index("rows"), lax.axis_index("cls") * width]).astype(jnp.int32)
    wanted = lax.all_to_all(fetch, "rows", split_axis=1, concat_axis=0, tiled=True)
    tabs = split(prior, tile_rows)
    blocks = blocks.reshape((-1,) + blocks.shape[2:])
    seeds = seeds.reshape(-1, LANES)
    temp = inv_temp.reshape(-1, LANES)

    sent = pick(me, wanted, tabs)
    gots = [across_core(sent[c][1], n) for c in range(chunks)]
    parcels = messages(sent[0][0], gots[0])
    arrived = [send(parcels, n)]
    (items, sizes), blocks, wide, begun = begin(
        me, links, counts, fetch, after(blocks, parcels, gots[1:]), seeds, temp, tabs
    )
    for c in range(1, chunks):
        parcels = [after(part, begun) for part in messages(sent[c][0], gots[c])]
        arrived.append(send(parcels, n))
    firsts, there = [], []
    for c in range(chunks):
        out, straight, across = step1(
            me, items, sizes, wanted, blocks, gots[c][0], arrived[c], after(begun[c], parcels)
        )
        got = across_core(across, n)
        parcels = messages(straight, got)
        firsts.append(out)
        there.append((got[0], send(parcels, n)))
    begun = own_part(me, items, sizes, blocks, after(seeds, parcels), firsts)
    expos, stats = [], []
    for c in range(chunks):
        near = near_part(items, sizes, blocks, *there[c], begun[c], n)
        live = min(LANES, width - c * LANES)
        expo, summary = step2(live, items, sizes, blocks, *there[c], near, wide)
        expos.append(expo)
        stats.append(
            [summary]
            + [
                lax.ppermute(summary, "cls", [(i, (i + k) % parts) for i in range(parts)])
                for k in range(1, parts)
            ]
        )
    pseudo, certainty = finish(expos, stats, width)
    return pseudo, certainty.reshape(-1)


def solution(mesh):
    return jax.shard_map(
        local,
        mesh=mesh,
        in_specs=(
            P("rows", "cls"),
            P("rows", None, None, None),
            P("rows", None),
            P("rows"),
            P("rows", None, None),
            P("rows"),
            P("rows"),
        ),
        out_specs=(P("rows", "cls"), P("rows")),
        check_vma=False,
    )
```

```python
import functools

import jax
import jax.numpy as jnp
from jax import lax
from jax.experimental import pallas as pl
from jax.experimental.pallas import tpu as pltpu
from jax.sharding import PartitionSpec as P

CLS = 1000
LANES = 128
GROUP = 16
blend = 0.8

SMEM = pl.BlockSpec(memory_space=pltpu.SMEM)
VMEM = pl.BlockSpec(memory_space=pltpu.VMEM)
ANY = pl.BlockSpec(memory_space=pl.ANY)
T_SHIFT, B_SHIFT = 20, 8


COST = pl.CostEstimate(flops=1, bytes_accessed=1, transcendentals=0)


def params(mib):
    return pltpu.CompilerParams(vmem_limit_bytes=mib << 20)


def held(shape, dtype):
    return pltpu.VMEM(shape, dtype)


def sds(shape, dtype):
    return jax.ShapeDtypeStruct(shape, dtype)


def split_kernel(prior_ref, *outs):
    width = prior_ref.shape[-1]
    for c, out in enumerate(outs):
        start = c * LANES
        live = min(LANES, width - start)
        out[:, :, :live] = prior_ref[:, :, start : start + live]
        if live < LANES:
            out[:, :, live:] = jnp.zeros(out.shape[:2] + (LANES - live,), out.dtype)


def split(prior, tile_rows):
    tiles = prior.reshape(-1, tile_rows, prior.shape[1])
    chunks = pl.cdiv(prior.shape[1], LANES)
    return pl.pallas_call(
        split_kernel,
        out_shape=[held((tiles.shape[0], tile_rows, LANES), prior.dtype)] * chunks,
        in_specs=[VMEM],
        out_specs=[VMEM] * chunks,
        compiler_params=params(8),
        name="split",
    )(tiles)


def fill_lists(room, index, links_ref, counts_ref, fetch_ref, items_ref, sizes_ref):
    own, slots = links_ref.shape
    n = fetch_ref.shape[0]
    mine = fetch_ref[index]

    def tile(t, sizes):
        def slot(j, sizes):
            v = links_ref[t, j]
            x = (v - own) ^ index
            is_own = jnp.logical_or(v < own, x == 0)
            is_near = jnp.logical_and(jnp.logical_not(is_own), x < n // 2)
            field = jnp.where(is_own, jnp.where(v < own, v, mine), x)
            place = jnp.where(
                is_own, sizes[0], jnp.where(is_near, 2 * room + sizes[1], 2 * room - 1 - sizes[2])
            )
            items_ref[place] = (t << T_SHIFT) + ((t * slots + j) << B_SHIFT) + field
            is_far = jnp.logical_not(jnp.logical_or(is_own, is_near))
            return tuple(
                size + kind.astype(jnp.int32) for size, kind in zip(sizes, (is_own, is_near, is_far))
            )

        return lax.fori_loop(0, counts_ref[t], slot, sizes)

    sizes = lax.fori_loop(0, own, tile, (jnp.int32(0),) * 3)
    for kind in range(3):
        sizes_ref[kind] = sizes[kind]
    sizes_ref[3] = fetch_ref[index ^ 1]

    def fill(i, carry):
        items_ref[sizes[0] + i] = own << T_SHIFT
        items_ref[2 * room + sizes[1] + i] = own << T_SHIFT
        items_ref[2 * room - sizes[2] - 1 - i] = own << T_SHIFT
        return carry

    lax.fori_loop(0, GROUP, fill, 0)


def groups_of(count):
    return (count + GROUP - 1) // GROUP


def own_list(room, sizes_ref):
    return 0, groups_of(sizes_ref[0])


def near_list(room, sizes_ref):
    return 2 * room, groups_of(sizes_ref[1])


def far_list(room, sizes_ref):
    groups = groups_of(sizes_ref[2])
    return 2 * room - groups * GROUP, groups


def both_lists(room, sizes_ref):
    return 2 * room - sizes_ref[2], groups_of(sizes_ref[1] + sizes_ref[2])


def ask_kernel(fetch_ref, out_ref):
    for i in range(fetch_ref.shape[0]):
        for j in range(2):
            out_ref[i, 0, j] = fetch_ref[i // 2 * 2 + j]


def ask(fetch):
    return pl.pallas_call(
        ask_kernel,
        out_shape=sds((fetch.shape[0], 1, 2), fetch.dtype),
        in_specs=[SMEM],
        out_specs=SMEM,
        name="ask",
    )(fetch)


def pick_kernel(chunks, me_ref, wanted_ref, *refs):
    tabs, neighbours, outs = refs[:chunks], refs[chunks : 2 * chunks], refs[2 * chunks :]
    index = me_ref[0]
    low = index & 1
    count = len(outs) // chunks
    for c in range(chunks):
        for k in range(count):
            to = index ^ (2 * k + 2)
            outs[c * count + k][0] = tabs[c][wanted_ref[to, 0, low]]
            outs[c * count + k][1] = neighbours[c][wanted_ref[to, 0, 1 - low]]


def pick(me, wanted, tabs, neighbours):
    chunks = len(tabs)
    count = wanted.shape[0] // 2 - 1
    outs = pl.pallas_call(
        functools.partial(pick_kernel, chunks),
        out_shape=[held((2,) + tabs[0].shape[1:], tabs[0].dtype)] * (chunks * count),
        in_specs=[SMEM, SMEM] + [VMEM] * (2 * chunks),
        out_specs=[VMEM] * (chunks * count),
        compiler_params=params(8),
        name="pick",
    )(me, wanted, *tabs, *neighbours)
    return [outs[c * count : (c + 1) * count] for c in range(chunks)]


def stay(arrays):
    return [pltpu.with_memory_space_constraint(array, pltpu.VMEM) for array in arrays]


def after(value, *others):
    return lax.optimization_barrier((value, others))[0]


def swap(value, n):
    return lax.ppermute(value, "rows", [(i, i ^ 1) for i in range(n)])


def across_core(across, n):
    half = across.shape[0] // 2
    late, early = swap(across[:half], n), swap(across[half:], n)
    return [late[k] for k in range(half)] + [early[k] for k in range(half)]


def messages(straight, got):
    return [jnp.stack([straight[k], got[k]]) for k in range(1, len(got))]


def send(parts, n):
    order = range(len(parts) - 1, -1, -1)
    arrived = [
        lax.ppermute(parts[k], "rows", [(i, i ^ (2 * k + 2)) for i in range(n)]) for k in order
    ]
    return arrived[::-1]


def run_list(which, items_ref, blocks, rhs, totals):
    first, groups = which
    low, high = (1 << B_SHIFT) - 1, (1 << (T_SHIFT - B_SHIFT)) - 1

    def step(g, carry):
        for i in range(GROUP):
            word = items_ref[first + g * GROUP + i]
            t = word >> T_SHIFT
            value = jnp.dot(
                blocks[(word >> B_SHIFT) & high],
                rhs(word & low),
                preferred_element_type=jnp.float32,
            )
            for c, total in enumerate(totals):
                total[t] += value[:, c * LANES : (c + 1) * LANES]
        return carry

    lax.fori_loop(0, groups, step, 0)


def column(ref, t, tile_rows):
    parts = tile_rows // LANES
    rows = [ref[pl.ds(t * parts + i, 1), :] for i in range(parts)]
    return jnp.concatenate(
        [jnp.broadcast_to(row, (LANES, LANES)).T for row in rows], axis=0
    )


def target_parts(me_ref, seeds_ref, parts):
    own, tile_rows = parts[0].shape[:2]
    share = (1.0 - blend) / blend
    lane = lax.broadcasted_iota(jnp.int32, parts[0].shape[1:], 1)
    for t in range(own):
        seeds = column(seeds_ref, t, tile_rows) - me_ref[1]
        for c, part in enumerate(parts):
            part[t] = jnp.where(seeds == lane + c * LANES, share, 0.0)


def start_totals(parts, totals):
    for part, total in zip(parts, totals):
        total[: part.shape[0]] = part[...]


def side_by_side(tabs):
    return lambda f: jnp.concatenate([tab[f] for tab in tabs], axis=1)


def load_kernel(
    room, me_ref, links_ref, counts_ref, fetch_ref, blocks_hbm, seeds_ref, temp_ref, *refs
):
    items_ref, sizes_ref, blocks, wide_ref = refs[:4]
    targets, sems = refs[4:-1], refs[-1]
    own, slots = links_ref.shape
    tile_rows = blocks.shape[1]
    groups = sems.shape[1]
    size = slots // groups

    def copy(t, g):
        return pltpu.make_async_copy(
            blocks_hbm.at[pl.ds(t * slots + g * size, size)],
            blocks.at[pl.ds(t * slots + g * size, size)],
            sems.at[t, g],
        )

    def used(t):
        return (counts_ref[t] + size - 1) // size

    def begin(t, carry):
        return lax.fori_loop(0, used(t), lambda g, c: (copy(t, g).start(), c)[1], carry)

    def ready(t, carry):
        return lax.fori_loop(0, used(t), lambda g, c: (copy(t, g).wait(), c)[1], carry)

    lax.fori_loop(0, own, begin, 0)
    fill_lists(room, me_ref[0], links_ref, counts_ref, fetch_ref, items_ref, sizes_ref)
    for t in range(own):
        wide_ref[t] = blend * column(temp_ref, t, tile_rows)
    target_parts(me_ref, seeds_ref, targets)
    lax.fori_loop(0, own, ready, 0)


def load(me, links, counts, fetch, blocks, seeds, temp, chunks):
    own, slots = links.shape
    tile_rows = blocks.shape[1]
    room = links.size + GROUP
    size = next(g for g in (4, 3, 2, 1) if slots % g == 0)
    wide = held((own, tile_rows, LANES), jnp.float32)
    out = pl.pallas_call(
        functools.partial(load_kernel, room),
        out_shape=[
            sds((3 * room,), jnp.int32),
            sds((4,), jnp.int32),
            held(blocks.shape, blocks.dtype),
        ]
        + [wide] * (1 + chunks),
        in_specs=[SMEM] * 4 + [ANY] + [VMEM] * 2,
        out_specs=[SMEM] * 2 + [VMEM] * (2 + chunks),
        scratch_shapes=[pltpu.SemaphoreType.DMA((own, slots // size))],
        compiler_params=params(8),
        cost_estimate=COST,
        name="load",
    )(me, links, counts, fetch, blocks, seeds, temp)
    return out[:2], out[2], out[3], out[4:]


def own_kernel(chunks, room, items_ref, sizes_ref, blocks, *refs):
    targets, tabs, totals = refs[:chunks], refs[chunks : 2 * chunks], refs[2 * chunks :]
    start_totals(targets, totals)
    run_list(own_list(room, sizes_ref), items_ref, blocks, side_by_side(tabs), totals)


def own_part(items, sizes, blocks, targets, tabs):
    own, tile_rows = tabs[0].shape[:2]
    chunks = len(tabs)
    return pl.pallas_call(
        functools.partial(own_kernel, chunks, items.shape[0] // 3),
        out_shape=[held((own + 1, tile_rows, LANES), jnp.float32)] * chunks,
        in_specs=[SMEM] * 2 + [VMEM] * (1 + 2 * chunks),
        out_specs=[VMEM] * chunks,
        compiler_params=params(8),
        cost_estimate=COST,
        name="own_part",
    )(items, sizes, blocks, *targets, *tabs)


def gather_field(near, far, beside, arrived, field):
    half = field.shape[0] // 2
    if near:
        field[1] = beside
    for k, one in enumerate(arrived):
        x = 2 * (k + 1)
        if near if x < half else far:
            field[x] = one[0]
            field[x + 1] = one[1]


def step1_kernel(
    links, room, me_ref, items_ref, sizes_ref, wanted_ref, blocks, neighbour, *refs
):
    arrived = refs[:links]
    begun, out, straight, across, field, total = refs[links:]
    own = out.shape[0]
    gather_field(True, True, neighbour[sizes_ref[3]], arrived, field)
    total[...] = begun[...]
    run_list(both_lists(room, sizes_ref), items_ref, blocks, lambda f: field[f], [total])
    for t in range(own):
        out[t] = (blend * total[t]).astype(out.dtype)
    index = me_ref[0]
    low = index & 1
    for x in range(field.shape[0]):
        (across if x % 2 else straight)[x // 2] = out[wanted_ref[index ^ x, 0, low]]


def step1(me, items, sizes, wanted, blocks, neighbour, arrived, begun):
    own, tile_rows = begun.shape[0] - 1, begun.shape[1]
    n = wanted.shape[0]
    dtype = neighbour.dtype
    half = held((n // 2, tile_rows, LANES), dtype)
    return pl.pallas_call(
        functools.partial(step1_kernel, len(arrived), items.shape[0] // 3),
        out_shape=[held((own, tile_rows, LANES), dtype), half, half],
        in_specs=[SMEM] * 4 + [VMEM] * (3 + len(arrived)),
        out_specs=[VMEM] * 3,
        scratch_shapes=[
            pltpu.VMEM((n, tile_rows, LANES), dtype),
            pltpu.VMEM(begun.shape, begun.dtype),
        ],
        compiler_params=params(12),
        cost_estimate=COST,
        name="step1",
    )(me, items, sizes, wanted, blocks, neighbour, *arrived, begun)


def near_kernel(links, room, items_ref, sizes_ref, blocks, beside, *refs):
    arrived = refs[:links]
    begun, total, field = refs[links:]
    gather_field(True, False, beside[...], arrived, field)
    total[...] = begun[...]
    run_list(near_list(room, sizes_ref), items_ref, blocks, lambda f: field[f], [total])


def near_part(items, sizes, blocks, beside, arrived, begun, n):
    tile_rows = begun.shape[1]
    return pl.pallas_call(
        functools.partial(near_kernel, len(arrived), items.shape[0] // 3),
        out_shape=held(begun.shape, begun.dtype),
        in_specs=[SMEM] * 2 + [VMEM] * (3 + len(arrived)),
        out_specs=VMEM,
        scratch_shapes=[pltpu.VMEM((n, tile_rows, LANES), beside.dtype)],
        compiler_params=params(8),
        cost_estimate=COST,
        name="near_part",
    )(items, sizes, blocks, beside, *arrived, begun)


def step2_kernel(links, live, near, room, items_ref, sizes_ref, blocks, beside, *refs):
    arrived = refs[:links]
    begun, wide_ref = refs[links : links + 2]
    *earlier, expo_ref, stats_ref, field, total = refs[links + 2 :]
    own, tile_rows = expo_ref.shape[:2]
    gather_field(near, True, beside[...], arrived, field)
    total[...] = begun[...]
    which = (both_lists if near else far_list)(room, sizes_ref)
    run_list(which, items_ref, blocks, lambda f: field[f], [total])
    parts = tile_rows // LANES
    last = stats_ref.shape[0] - 1
    if earlier:
        stats_ref[:last] = earlier[0][...]
    for t in range(own):
        logits = wide_ref[t] * total[t]
        lane = lax.broadcasted_iota(jnp.int32, logits.shape, 1)
        if live < LANES:
            top = jnp.max(jnp.where(lane < live, logits, -jnp.inf), axis=1, keepdims=True)
            shifted = jnp.where(lane < live, logits - top, 0.0)
            expo = jnp.where(lane < live, jnp.exp(shifted), 0.0)
        else:
            top = jnp.max(logits, axis=1, keepdims=True)
            shifted = logits - top
            expo = jnp.exp(shifted)
        sums = jnp.sum(expo, axis=1, keepdims=True)
        moments = jnp.sum(expo * shifted, axis=1, keepdims=True)
        expo_ref[t] = expo
        summary = jnp.where(lane == 0, top, jnp.where(lane == 1, sums, moments))
        for i in range(parts):
            flat = summary[i * LANES : (i + 1) * LANES, :].T
            for q in range(3):
                stats_ref[last, q, t * parts + i : t * parts + i + 1, :] = flat[q : q + 1]


def step2(live, near, items, sizes, blocks, beside, arrived, begun, wide, earlier):
    own, tile_rows = begun.shape[0] - 1, begun.shape[1]
    n = 2 * (len(arrived) + 1)
    before = () if earlier is None else (earlier,)
    count = 1 + (earlier.shape[0] if before else 0)
    return pl.pallas_call(
        functools.partial(step2_kernel, len(arrived), live, near, items.shape[0] // 3),
        out_shape=[
            held((own, tile_rows, LANES), jnp.float32),
            held((count, 3, own * tile_rows // LANES, LANES), jnp.float32),
        ],
        in_specs=[SMEM] * 2 + [VMEM] * (4 + len(arrived) + len(before)),
        out_specs=[VMEM] * 2,
        scratch_shapes=[
            pltpu.VMEM((n, tile_rows, LANES), beside.dtype),
            pltpu.VMEM(begun.shape, begun.dtype),
        ],
        compiler_params=params(12),
        cost_estimate=COST,
        name="step2",
    )(items, sizes, blocks, beside, *arrived, begun, wide, *before)


def finish_kernel(chunks, parts, *refs):
    expos, stats = refs[:chunks], refs[chunks : chunks + parts]
    pseudo_ref, certainty_ref, scale_ref = refs[chunks + parts :]
    own, tile_rows = expos[0].shape[:2]
    width = pseudo_ref.shape[1]
    every = [(s, c) for s in stats for c in range(chunks)]
    top = functools.reduce(jnp.maximum, [s[c, 0] for s, c in every])
    totals, moments, scales = 0.0, 0.0, []
    for s, c in every:
        delta = s[c, 0] - top
        scale = jnp.exp(delta)
        scales.append(scale)
        totals += scale * s[c, 1]
        moments += scale * (s[c, 2] + delta * s[c, 1])
    certainty_ref[...] = 1.0 - (jnp.log(totals) - moments / totals) / jnp.log(jnp.float32(CLS))
    inverse = 1.0 / totals
    for c in range(chunks):
        scale_ref[c] = scales[c] * inverse
    for t in range(own):
        span = slice(t * tile_rows, (t + 1) * tile_rows)
        for c in range(chunks):
            start = c * LANES
            live = min(LANES, width - start)
            value = expos[c][t] * column(scale_ref.at[c], t, tile_rows)
            pseudo_ref[span, start : start + live] = value[:, :live].astype(pseudo_ref.dtype)


def finish(expos, stats, width):
    own, tile_rows = expos[0].shape[:2]
    rows = own * tile_rows
    chunks, parts = len(expos), len(stats)
    return pl.pallas_call(
        functools.partial(finish_kernel, chunks, parts),
        out_shape=[sds((rows, width), jnp.bfloat16), sds((rows // LANES, LANES), jnp.float32)],
        in_specs=[VMEM] * (chunks + parts),
        out_specs=[VMEM] * 2,
        scratch_shapes=[pltpu.VMEM((chunks, rows // LANES, LANES), jnp.float32)],
        compiler_params=params(12),
        name="finish",
    )(*expos, *stats)


def local(prior, blocks, links, counts, fetch, seeds, inv_temp):
    width = prior.shape[1]
    tile_rows = blocks.shape[2]
    n = lax.axis_size("rows")
    parts = lax.axis_size("cls")
    chunks = pl.cdiv(width, LANES)
    me = jnp.stack([lax.axis_index("rows"), lax.axis_index("cls") * width]).astype(jnp.int32)
    fetch = fetch.reshape(n)
    wanted = lax.all_to_all(ask(fetch), "rows", split_axis=0, concat_axis=0, tiled=True)
    tabs = stay(split(prior, tile_rows))
    neighbours = stay(split(swap(prior, n), tile_rows))
    blocks = blocks.reshape((-1,) + blocks.shape[2:])
    seeds = seeds.reshape(-1, LANES)
    temp = inv_temp.reshape(-1, LANES)

    sent = pick(me, wanted, tabs, neighbours)
    arrived = [send(sent[0], n)]
    (items, sizes), blocks, wide, targets = load(
        me, links, counts, fetch, after(blocks, sent), seeds, temp, chunks
    )
    parcels = []
    for c in range(1, chunks):
        parcels = [after(part, sizes) for part in sent[c]]
        arrived.append(send(parcels, n))
    begun = own_part(items, sizes, after(blocks, parcels), targets, tabs)
    firsts, there = [], []
    for c in range(chunks):
        out, straight, across = step1(
            me, items, sizes, wanted, blocks, neighbours[c], arrived[c], after(begun[c], parcels)
        )
        got = across_core(across, n)
        parcels = messages(straight, got)
        firsts.append(out)
        there.append((got[0], send(parcels, n)))
    begun = own_part(items, sizes, after(blocks, parcels), targets, firsts)
    expos, stats = [], None
    for c in range(chunks):
        near = c < chunks - 1
        total = begun[c]
        if not near:
            total = near_part(items, sizes, blocks, *there[c], total, n)
        live = min(LANES, width - c * LANES)
        expo, stats = step2(
            live, near, items, sizes, blocks, *there[c], total, wide, stats
        )
        expos.append(expo)
    stats = [stats] + [
        lax.ppermute(stats, "cls", [(i, (i + k) % parts) for i in range(parts)])
        for k in range(1, parts)
    ]
    pseudo, certainty = finish(expos, stats, width)
    return pseudo, certainty.reshape(-1)


def solution(mesh):
    return jax.shard_map(
        local,
        mesh=mesh,
        in_specs=(
            P("rows", "cls"),
            P("rows", None, None, None),
            P("rows", None),
            P("rows"),
            P("rows", None, None),
            P("rows"),
            P("rows"),
        ),
        out_specs=(P("rows", "cls"), P("rows")),
        check_vma=False,
    )
```

```python
import functools

import jax
import jax.numpy as jnp
from jax import lax
from jax.experimental import pallas as pl
from jax.experimental.pallas import tpu as pltpu
from jax.sharding import PartitionSpec as P

CLS = 1000
LANES = 128
GROUP = 16
blend = 0.8

SMEM = pl.BlockSpec(memory_space=pltpu.SMEM)
VMEM = pl.BlockSpec(memory_space=pltpu.VMEM)
HBM = pl.BlockSpec(memory_space=pltpu.HBM)
T_SHIFT, B_SHIFT = 20, 8


COST = pl.CostEstimate(flops=1, bytes_accessed=1, transcendentals=0)


PARAMS = pltpu.CompilerParams(vmem_limit_bytes=8 << 20)


def held(shape, dtype):
    return pltpu.VMEM(shape, dtype)


def sds(shape, dtype):
    return jax.ShapeDtypeStruct(shape, dtype)


def put_chunk(out, value, chunk):
    start = chunk * LANES
    live = min(LANES, value.shape[-1] - start)
    out[..., :live] = value[..., start : start + live]
    if live < LANES:
        out[..., live:] = jnp.zeros(value.shape[:-1] + (LANES - live,), out.dtype)


def fill_lists(room, index, links_ref, counts_ref, fetch_ref, items_ref, sizes_ref):
    own, slots = links_ref.shape
    n = fetch_ref.shape[0]
    mine = fetch_ref[index]

    def tile(t, sizes):
        def slot(j, sizes):
            v = links_ref[t, j]
            x = (v - own) ^ index
            is_own = jnp.logical_or(v < own, x == 0)
            is_near = jnp.logical_and(jnp.logical_not(is_own), x < n // 2)
            field = jnp.where(is_own, jnp.where(v < own, v, mine), x)
            place = jnp.where(
                is_own, sizes[0], jnp.where(is_near, 2 * room + sizes[1], 2 * room - 1 - sizes[2])
            )
            items_ref[place] = (t << T_SHIFT) + ((t * slots + j) << B_SHIFT) + field
            is_far = jnp.logical_not(jnp.logical_or(is_own, is_near))
            return tuple(
                size + kind.astype(jnp.int32) for size, kind in zip(sizes, (is_own, is_near, is_far))
            )

        return lax.fori_loop(0, counts_ref[t], slot, sizes)

    sizes = lax.fori_loop(0, own, tile, (jnp.int32(0),) * 3)
    for kind in range(3):
        sizes_ref[kind] = sizes[kind]
    sizes_ref[3] = fetch_ref[index ^ 1]

    def fill(i, carry):
        items_ref[sizes[0] + i] = own << T_SHIFT
        items_ref[2 * room + sizes[1] + i] = own << T_SHIFT
        items_ref[2 * room - sizes[2] - 1 - i] = own << T_SHIFT
        return carry

    lax.fori_loop(0, GROUP, fill, 0)


def groups_of(count):
    return (count + GROUP - 1) // GROUP


def own_list(room, sizes_ref):
    return 0, groups_of(sizes_ref[0])


def near_list(room, sizes_ref):
    return 2 * room, groups_of(sizes_ref[1])


def far_list(room, sizes_ref):
    groups = groups_of(sizes_ref[2])
    return 2 * room - groups * GROUP, groups


def both_lists(room, sizes_ref):
    return 2 * room - sizes_ref[2], groups_of(sizes_ref[1] + sizes_ref[2])


def near_bound(n):
    return max(1, n // 4)


def split_kernel(prior_ref, *outs):
    for c, out in enumerate(outs):
        put_chunk(out, prior_ref[...], c)


def split(prior, chunks):
    return pl.pallas_call(
        split_kernel,
        out_shape=[held(prior.shape[:2] + (LANES,), prior.dtype)] * chunks,
        in_specs=[VMEM],
        out_specs=[VMEM] * chunks,
        compiler_params=PARAMS,
        name="split",
    )(prior)


def pick_kernel(chunks, me_ref, fetch_ref, *refs):
    n = fetch_ref.shape[0]
    count = n // 2 - 1
    lists = (fetch_ref,) + refs[:count]
    tabs, neighbours = refs[count : count + chunks], refs[count + chunks : count + 2 * chunks]
    asked_ref, *outs = refs[count + 2 * chunks :]
    besides, outs = outs[:chunks], outs[chunks:]
    index = me_ref[0]
    first = near_bound(n)
    for c in range(chunks):
        besides[c][...] = neighbours[c][fetch_ref[index ^ 1]]
    for k in range(1, n // 2):
        mine, other = lists[k][index], lists[k][index ^ 1]
        for c in range(chunks):
            if k < first:
                out, at = outs[k - 1], 2 * c
            else:
                out, at = outs[first - 1 + c * (n // 2 - first) + k - first], 0
            out[at] = tabs[c][mine]
            out[at + 1] = neighbours[c][other]
    for k, one in enumerate(lists):
        for j in range(n):
            asked_ref[k, j] = one[j]


def pick(me, fetch, lists, tabs, neighbours):
    n = fetch.shape[0]
    chunks = len(tabs)
    first = near_bound(n)
    tile, dtype = tabs[0].shape[1:], tabs[0].dtype
    near, far = first - 1, n // 2 - first
    outs = pl.pallas_call(
        functools.partial(pick_kernel, chunks),
        out_shape=[sds((n // 2, n), fetch.dtype)]
        + [held(tile, dtype)] * chunks
        + [held((2 * chunks,) + tile, dtype)] * near
        + [held((2,) + tile, dtype)] * (chunks * far),
        in_specs=[SMEM] * (2 + len(lists)) + [VMEM] * (2 * chunks),
        out_specs=[SMEM] + [VMEM] * (chunks + near + chunks * far),
        compiler_params=PARAMS,
        name="pick",
    )(me, fetch, *lists, *tabs, *neighbours)
    far_parts = outs[1 + chunks + near :]
    return (
        outs[0],
        outs[1 : 1 + chunks],
        outs[1 + chunks : 1 + chunks + near],
        [far_parts[c * far : (c + 1) * far] for c in range(chunks)],
    )


def after(value, *others):
    return lax.optimization_barrier((value, others))[0]


def swap(value, n):
    return lax.ppermute(value, "rows", [(i, i ^ 1) for i in range(n)])


def send(parts, ks, n):
    return [
        lax.ppermute(part, "rows", [(i, i ^ (2 * k)) for i in range(n)])
        for part, k in zip(parts, ks)
    ]


def run_list(which, items_ref, blocks, rhs, totals, ready=None):
    first, groups = which
    own = totals[0].shape[0] - 1
    low, high = (1 << B_SHIFT) - 1, (1 << (T_SHIFT - B_SHIFT)) - 1

    def step(g, waited):
        at = first + g * GROUP
        if ready is not None:
            last = jnp.minimum(items_ref[at + GROUP - 1] >> T_SHIFT, own - 1) + 1
            lax.fori_loop(waited, last, ready, 0)
            waited = jnp.maximum(waited, last)
        for i in range(GROUP):
            word = items_ref[at + i]
            t = word >> T_SHIFT
            value = jnp.dot(
                blocks[(word >> B_SHIFT) & high],
                rhs(word & low),
                preferred_element_type=jnp.float32,
            )
            for c, total in enumerate(totals):
                total[t] += value[:, c * LANES : (c + 1) * LANES]
        return waited

    waited = lax.fori_loop(0, groups, step, jnp.int32(0))
    if ready is not None:
        lax.fori_loop(waited, own, ready, 0)


def column(ref, t, tile_rows):
    parts = tile_rows // LANES
    rows = [ref[pl.ds(t * parts + i, 1), :] for i in range(parts)]
    return jnp.concatenate(
        [jnp.broadcast_to(row, (LANES, LANES)).T for row in rows], axis=0
    )


def start_totals(me_ref, seeds_ref, totals):
    own, tile_rows = totals[0].shape[0] - 1, totals[0].shape[1]
    share = (1.0 - blend) / blend
    lane = lax.broadcasted_iota(jnp.int32, totals[0].shape[1:], 1)
    for t in range(own):
        seeds = column(seeds_ref, t, tile_rows) - me_ref[1]
        for c, total in enumerate(totals):
            total[t] = jnp.where(seeds == lane + c * LANES, share, 0.0)


def side_by_side(tabs):
    return lambda f: jnp.concatenate([tab[f] for tab in tabs], axis=1)


def prepare_kernel(room, me_ref, links_ref, counts_ref, fetch_ref, items_ref, sizes_ref):
    fill_lists(room, me_ref[0], links_ref, counts_ref, fetch_ref, items_ref, sizes_ref)


def prepare(me, links, counts, fetch):
    room = links.size + GROUP
    return pl.pallas_call(
        functools.partial(prepare_kernel, room),
        out_shape=[sds((3 * room,), jnp.int32), sds((4,), jnp.int32)],
        in_specs=[SMEM] * 4,
        out_specs=[SMEM] * 2,
        compiler_params=PARAMS,
        cost_estimate=COST,
        name="prepare",
    )(me, links, counts, fetch)


def begin_kernel(
    room, me_ref, items_ref, sizes_ref, counts_ref, blocks_hbm, prior, seeds_ref, blocks, *refs
):
    *totals, stage, tab, sems, prior_sem = refs
    own, groups = sems.shape
    slots = blocks.shape[0] // own
    size = slots // groups
    load = pltpu.make_async_copy(prior, stage, prior_sem)
    load.start()

    def copy(t, g):
        span = pl.ds(t * slots + g * size, size)
        return pltpu.make_async_copy(blocks_hbm.at[span], blocks.at[span], sems.at[t, g])

    def used(t):
        return (counts_ref[t] + size - 1) // size

    def begin(t, carry):
        return lax.fori_loop(0, used(t), lambda g, c: (copy(t, g).start(), c)[1], carry)

    def ready(t, carry):
        return lax.fori_loop(0, used(t), lambda g, c: (copy(t, g).wait(), c)[1], carry)

    lax.fori_loop(0, own, begin, 0)
    start_totals(me_ref, seeds_ref, totals)
    load.wait()
    for c in range(len(totals)):
        put_chunk(tab.at[:, :, pl.ds(c * LANES, LANES)], stage[...], c)
    run_list(own_list(room, sizes_ref), items_ref, blocks, lambda f: tab[f], totals, ready)


def begin(me, items, sizes, counts, blocks, prior, seeds, chunks):
    own, tile_rows = prior.shape[:2]
    slots = blocks.shape[0] // own
    size = next(g for g in (4, 3, 2, 1) if slots % g == 0)
    out = pl.pallas_call(
        functools.partial(begin_kernel, items.shape[0] // 3),
        out_shape=[held(blocks.shape, blocks.dtype)]
        + [held((own + 1, tile_rows, LANES), jnp.float32)] * chunks,
        in_specs=[SMEM] * 4 + [HBM] * 2 + [VMEM],
        out_specs=[VMEM] * (1 + chunks),
        scratch_shapes=[
            pltpu.VMEM(prior.shape, prior.dtype),
            pltpu.VMEM((own, tile_rows, chunks * LANES), prior.dtype),
            pltpu.SemaphoreType.DMA((own, slots // size)),
            pltpu.SemaphoreType.DMA,
        ],
        compiler_params=PARAMS,
        cost_estimate=COST,
        name="begin",
    )(me, items, sizes, counts, blocks, prior, seeds)
    return out[0], out[1:]


def own_kernel(chunks, room, me_ref, items_ref, sizes_ref, blocks, seeds_ref, temp_ref, *refs):
    tabs, wide_ref, totals = refs[:chunks], refs[chunks], refs[chunks + 1 :]
    start_totals(me_ref, seeds_ref, totals)
    own, tile_rows = wide_ref.shape[:2]
    for t in range(own):
        wide_ref[t] = blend * column(temp_ref, t, tile_rows)
    run_list(own_list(room, sizes_ref), items_ref, blocks, side_by_side(tabs), totals)


def own_part(me, items, sizes, blocks, seeds, temp, tabs):
    own, tile_rows = tabs[0].shape[:2]
    chunks = len(tabs)
    out = pl.pallas_call(
        functools.partial(own_kernel, chunks, items.shape[0] // 3),
        out_shape=[held((own, tile_rows, LANES), jnp.float32)]
        + [held((own + 1, tile_rows, LANES), jnp.float32)] * chunks,
        in_specs=[SMEM] * 3 + [VMEM] * (3 + chunks),
        out_specs=[VMEM] * (1 + chunks),
        compiler_params=PARAMS,
        cost_estimate=COST,
        name="own_part",
    )(me, items, sizes, blocks, seeds, temp, *tabs)
    return out[0], out[1:]


def put_near(chunk, near, field):
    for k, one in enumerate(near):
        for j in range(2):
            field[2 * (k + 1) + j] = one[2 * chunk + j]


def put_far(first, far, field):
    for k, one in enumerate(far):
        for j in range(2):
            field[2 * (first + k) + j] = one[j]


def put_pairs(first, arrived, got, field):
    for i, (one, other) in enumerate(zip(arrived, got)):
        field[2 * (first + i)] = one[0]
        field[2 * (first + i) + 1] = other[0]


def step1_kernel(
    nears, fars, chunk, room, me_ref, items_ref, sizes_ref, asked_ref, beside_ref, blocks, *refs
):
    tile, near, far = refs[0], refs[1 : 1 + nears], refs[1 + nears : 1 + nears + fars]
    begun, out, beside_tile, *messages, field, total = refs[1 + nears + fars :]
    own = out.shape[0]
    field[1] = tile[...]
    put_near(chunk, near, field)
    put_far(nears + 1, far, field)
    total[...] = begun[...]
    run_list(both_lists(room, sizes_ref), items_ref, blocks, lambda f: field[f], [total])
    for t in range(own):
        out[t] = (blend * total[t]).astype(out.dtype)
    index = me_ref[0]
    beside_tile[0] = out[beside_ref[0, index]]
    for k, message in enumerate(messages):
        message[0] = out[asked_ref[k + 1, index]]
        message[1] = out[beside_ref[k + 1, index]]


def step1(chunk, me, items, sizes, asked, beside, blocks, tile, near, far, begun):
    own, tile_rows = begun.shape[0] - 1, begun.shape[1]
    n = asked.shape[1]
    dtype = tile.dtype
    count = n // 2 - 1
    out = pl.pallas_call(
        functools.partial(step1_kernel, len(near), len(far), chunk, items.shape[0] // 3),
        out_shape=[
            held((own, tile_rows, LANES), dtype),
            held((1, tile_rows, LANES), dtype),
        ]
        + [held((2, tile_rows, LANES), dtype)] * count,
        in_specs=[SMEM] * 5 + [VMEM] * (3 + len(near) + len(far)),
        out_specs=[VMEM] * (2 + count),
        scratch_shapes=[
            pltpu.VMEM((n, tile_rows, LANES), dtype),
            pltpu.VMEM(begun.shape, begun.dtype),
        ],
        compiler_params=PARAMS,
        cost_estimate=COST,
        name="step1",
    )(me, items, sizes, asked, beside, blocks, tile, *near, *far, begun)
    return out[0], out[1], out[2:]


def near_kernel(nears, room, items_ref, sizes_ref, blocks, *refs):
    got, near, (_, total, field) = refs[: nears + 1], refs[nears + 1 : -3], refs[-3:]
    field[1] = got[0][0]
    put_pairs(1, near, got[1:], field)
    run_list(near_list(room, sizes_ref), items_ref, blocks, lambda f: field[f], [total])


def near_part(items, sizes, blocks, got, near, begun):
    tile_rows = begun.shape[1]
    return pl.pallas_call(
        functools.partial(near_kernel, len(near), items.shape[0] // 3),
        out_shape=held(begun.shape, begun.dtype),
        in_specs=[SMEM] * 2 + [VMEM] * (3 + 2 * len(near)),
        out_specs=VMEM,
        input_output_aliases={4 + 2 * len(near): 0},
        scratch_shapes=[pltpu.VMEM((2 * (len(near) + 1), tile_rows, LANES), got[0].dtype)],
        compiler_params=PARAMS,
        cost_estimate=COST,
        name="near_part",
    )(items, sizes, blocks, *got, *near, begun)


def step2_kernel(gots, count, live, whole, room, items_ref, sizes_ref, blocks, *refs):
    got, arrived = refs[:gots], refs[gots : gots + count]
    begun, wide_ref = refs[gots + count : gots + count + 2]
    *earlier, expo_ref, stats_ref, field, total = refs[gots + count + 2 :]
    own, tile_rows = expo_ref.shape[:2]
    if whole:
        field[1] = got[0][0]
        put_far(1, arrived, field)
    else:
        put_pairs(field.shape[0] // 2 - count, arrived, got, field)
    total[...] = begun[...]
    which = (both_lists if whole else far_list)(room, sizes_ref)
    run_list(which, items_ref, blocks, lambda f: field[f], [total])
    parts = tile_rows // LANES
    last = stats_ref.shape[0] - 1
    if earlier:
        stats_ref[:last] = earlier[0][...]
    for t in range(own):
        logits = wide_ref[t] * total[t]
        lane = lax.broadcasted_iota(jnp.int32, logits.shape, 1)
        if live < LANES:
            top = jnp.max(jnp.where(lane < live, logits, -jnp.inf), axis=1, keepdims=True)
            shifted = jnp.where(lane < live, logits - top, 0.0)
            expo = jnp.where(lane < live, jnp.exp(shifted), 0.0)
        else:
            top = jnp.max(logits, axis=1, keepdims=True)
            shifted = logits - top
            expo = jnp.exp(shifted)
        sums = jnp.sum(expo, axis=1, keepdims=True)
        moments = jnp.sum(expo * shifted, axis=1, keepdims=True)
        expo_ref[t] = expo
        summary = jnp.where(lane == 0, top, jnp.where(lane == 1, sums, moments))
        for i in range(parts):
            flat = summary[i * LANES : (i + 1) * LANES, :].T
            for q in range(3):
                stats_ref[last, q, t * parts + i : t * parts + i + 1, :] = flat[q : q + 1]


def step2(live, whole, n, items, sizes, blocks, got, arrived, begun, wide, earlier):
    own, tile_rows = begun.shape[0] - 1, begun.shape[1]
    before = () if earlier is None else (earlier,)
    count = 1 + (earlier.shape[0] if before else 0)
    return pl.pallas_call(
        functools.partial(
            step2_kernel, len(got), len(arrived), live, whole, items.shape[0] // 3
        ),
        out_shape=[
            held((own, tile_rows, LANES), jnp.float32),
            held((count, 3, own * tile_rows // LANES, LANES), jnp.float32),
        ],
        in_specs=[SMEM] * 2 + [VMEM] * (3 + len(got) + len(arrived) + len(before)),
        out_specs=[VMEM] * 2,
        scratch_shapes=[
            pltpu.VMEM((n, tile_rows, LANES), got[0].dtype),
            pltpu.VMEM(begun.shape, begun.dtype),
        ],
        compiler_params=PARAMS,
        cost_estimate=COST,
        name="step2",
    )(items, sizes, blocks, *got, *arrived, begun, wide, *before)


def finish_kernel(chunks, parts, *refs):
    expos, stats = refs[:chunks], refs[chunks : chunks + parts]
    pseudo_ref, certainty_ref, scale_ref = refs[chunks + parts :]
    own, tile_rows = expos[0].shape[:2]
    width = pseudo_ref.shape[1]
    every = [(s, c) for s in stats for c in range(chunks)]
    top = functools.reduce(jnp.maximum, [s[c, 0] for s, c in every])
    totals, moments, scales = 0.0, 0.0, []
    for s, c in every:
        delta = s[c, 0] - top
        scale = jnp.exp(delta)
        scales.append(scale)
        totals += scale * s[c, 1]
        moments += scale * (s[c, 2] + delta * s[c, 1])
    certainty_ref[...] = 1.0 - (jnp.log(totals) - moments / totals) / jnp.log(jnp.float32(CLS))
    inverse = 1.0 / totals
    for c in range(chunks):
        scale_ref[c] = scales[c] * inverse
    for t in range(own):
        span = slice(t * tile_rows, (t + 1) * tile_rows)
        for c in range(chunks):
            start = c * LANES
            live = min(LANES, width - start)
            value = expos[c][t] * column(scale_ref.at[c], t, tile_rows)
            pseudo_ref[span, start : start + live] = value[:, :live].astype(pseudo_ref.dtype)


def finish(expos, stats, width):
    own, tile_rows = expos[0].shape[:2]
    rows = own * tile_rows
    chunks, parts = len(expos), len(stats)
    return pl.pallas_call(
        functools.partial(finish_kernel, chunks, parts),
        out_shape=[sds((rows, width), jnp.bfloat16), sds((rows // LANES, LANES), jnp.float32)],
        in_specs=[VMEM] * (chunks + parts),
        out_specs=[VMEM] * 2,
        scratch_shapes=[pltpu.VMEM((chunks, rows // LANES, LANES), jnp.float32)],
        compiler_params=PARAMS,
        name="finish",
    )(*expos, *stats)


def local(prior, blocks, links, counts, fetch, seeds, inv_temp):
    width = prior.shape[1]
    tile_rows = blocks.shape[2]
    n = lax.axis_size("rows")
    parts = lax.axis_size("cls")
    chunks = pl.cdiv(width, LANES)
    me = jnp.stack([lax.axis_index("rows"), lax.axis_index("cls") * width]).astype(jnp.int32)
    fetch = fetch.reshape(n)
    first = near_bound(n)
    near_ks, far_ks = range(1, first), range(first, n // 2)
    neighbour = swap(prior, n).reshape(-1, tile_rows, width)
    prior = prior.reshape(-1, tile_rows, width)
    lists = send([fetch] * (n // 2 - 1), range(1, n // 2), n)
    tabs, neighbours = split(prior, chunks), split(neighbour, chunks)
    blocks = blocks.reshape((-1,) + blocks.shape[2:])
    seeds = seeds.reshape(-1, LANES)
    temp = inv_temp.reshape(-1, LANES)

    asked, tiles, near_sent, far_sent = pick(me, fetch, lists, tabs, neighbours)
    beside = swap(asked, n)
    near = send(near_sent, near_ks, n)
    far = [send(far_sent[0], far_ks, n)]
    items, sizes = prepare(me, links, counts, after(fetch, near_sent, far_sent))
    parcels = []
    for c in range(1, chunks):
        parcels = [after(part, sizes, beside) for part in far_sent[c]]
        far.append(send(parcels, far_ks, n))
    blocks, begun = begin(
        me, items, sizes, counts, after(blocks, parcels), prior, seeds, chunks
    )
    firsts, there = [], []
    ks = range(1, n // 2)
    for c in range(chunks):
        out, tile, parcels = step1(
            c, me, items, sizes, asked, beside, blocks, tiles[c], near, far[c],
            after(begun[c], parcels),
        )
        firsts.append(out)
        if c < chunks - 1:
            seconds = [swap(part[1:], n) for part in parcels]
            parcels = [jnp.concatenate([p[:1], q]) for p, q in zip(parcels, seconds)]
            tile = swap(after(tile, parcels), n)
        elif there:
            parcels = [after(part, there[-1][1][: first - 1]) for part in parcels]
        there.append((tile, send(parcels[::-1], ks[::-1], n)[::-1]))
    wide, begun = own_part(me, items, sizes, blocks, after(seeds, parcels), temp, firsts)
    expos, stats = [], None
    for c in range(chunks):
        live = min(LANES, width - c * LANES)
        (tile, here), total = there[c], begun[c]
        if c < chunks - 1:
            got = [tile]
        else:
            near, here = here[: first - 1], here[first - 1 :]
            tile = after(tile, near)
            got = [swap(part, n) for part in [tile] + [part[1:] for part in near]]
            total = near_part(items, sizes, blocks, got, near, total)
            if stats is not None:
                here = [after(part, stats) for part in here]
            got = [swap(part[1:], n) for part in here]
        expo, stats = step2(
            live, c < chunks - 1, n, items, sizes, blocks, got, here, total, wide, stats
        )
        expos.append(expo)
    stats = [stats] + [
        lax.ppermute(stats, "cls", [(i, (i + k) % parts) for i in range(parts)])
        for k in range(1, parts)
    ]
    pseudo, certainty = finish(expos, stats, width)
    return pseudo, certainty.reshape(-1)


def solution(mesh):
    return jax.shard_map(
        local,
        mesh=mesh,
        in_specs=(
            P("rows", "cls"),
            P("rows", None, None, None),
            P("rows", None),
            P("rows"),
            P("rows", None, None),
            P("rows"),
            P("rows"),
        ),
        out_specs=(P("rows", "cls"), P("rows")),
        check_vma=False,
    )
```

```python
import functools

import jax
import jax.numpy as jnp
from jax import lax
from jax.experimental import pallas as pl
from jax.experimental.pallas import tpu as pltpu
from jax.sharding import PartitionSpec as P

CLS = 1000
LANES = 128
GROUP = 16
blend = 0.8

SMEM = pl.BlockSpec(memory_space=pltpu.SMEM)
VMEM = pl.BlockSpec(memory_space=pltpu.VMEM)
HBM = pl.BlockSpec(memory_space=pltpu.HBM)
T_SHIFT, B_SHIFT = 20, 8


COST = pl.CostEstimate(flops=1, bytes_accessed=1, transcendentals=0)


PARAMS = pltpu.CompilerParams(vmem_limit_bytes=8 << 20)


def held(shape, dtype):
    return pltpu.VMEM(shape, dtype)


def sds(shape, dtype):
    return jax.ShapeDtypeStruct(shape, dtype)


def put_chunk(out, value, chunk):
    start = chunk * LANES
    live = min(LANES, value.shape[-1] - start)
    out[..., :live] = value[..., start : start + live]
    if live < LANES:
        out[..., live:] = jnp.zeros(value.shape[:-1] + (LANES - live,), out.dtype)


def fill_lists(room, index, links_ref, counts_ref, fetch_ref, items_ref, sizes_ref):
    own, slots = links_ref.shape
    n = fetch_ref.shape[0]
    mine = fetch_ref[index]

    def tile(t, sizes):
        def slot(j, sizes):
            v = links_ref[t, j]
            x = (v - own) ^ index
            is_own = jnp.logical_or(v < own, x == 0)
            is_near = jnp.logical_and(jnp.logical_not(is_own), x < n // 2)
            field = jnp.where(is_own, jnp.where(v < own, v, mine), x)
            place = jnp.where(
                is_own, sizes[0], jnp.where(is_near, 2 * room + sizes[1], 2 * room - 1 - sizes[2])
            )
            items_ref[place] = (t << T_SHIFT) + ((t * slots + j) << B_SHIFT) + field
            is_far = jnp.logical_not(jnp.logical_or(is_own, is_near))
            return tuple(
                size + kind.astype(jnp.int32) for size, kind in zip(sizes, (is_own, is_near, is_far))
            )

        return lax.fori_loop(0, counts_ref[t], slot, sizes)

    sizes = lax.fori_loop(0, own, tile, (jnp.int32(0),) * 3)
    for kind in range(3):
        sizes_ref[kind] = sizes[kind]
    sizes_ref[3] = fetch_ref[index ^ 1]

    def fill(i, carry):
        items_ref[sizes[0] + i] = own << T_SHIFT
        items_ref[2 * room + sizes[1] + i] = own << T_SHIFT
        items_ref[2 * room - sizes[2] - 1 - i] = own << T_SHIFT
        return carry

    lax.fori_loop(0, GROUP, fill, 0)


def groups_of(count):
    return (count + GROUP - 1) // GROUP


def own_list(room, sizes_ref):
    return 0, groups_of(sizes_ref[0])


def near_list(room, sizes_ref):
    return 2 * room, groups_of(sizes_ref[1])


def far_list(room, sizes_ref):
    groups = groups_of(sizes_ref[2])
    return 2 * room - groups * GROUP, groups


def both_lists(room, sizes_ref):
    return 2 * room - sizes_ref[2], groups_of(sizes_ref[1] + sizes_ref[2])


def near_bound(n):
    return max(1, n // 4)


def split_kernel(prior_ref, *outs):
    for c, out in enumerate(outs):
        put_chunk(out, prior_ref[...], c)


def split(prior, chunks):
    return pl.pallas_call(
        split_kernel,
        out_shape=[held(prior.shape[:2] + (LANES,), prior.dtype)] * chunks,
        in_specs=[VMEM],
        out_specs=[VMEM] * chunks,
        compiler_params=PARAMS,
        name="split",
    )(prior)


def pick_kernel(chunks, me_ref, fetch_ref, *refs):
    n = fetch_ref.shape[0]
    count = n // 2 - 1
    lists = (fetch_ref,) + refs[:count][::-1]
    tabs, neighbours = refs[count : count + chunks], refs[count + chunks : count + 2 * chunks]
    asked_ref, *outs = refs[count + 2 * chunks :]
    besides, outs = outs[:chunks], outs[chunks:]
    index = me_ref[0]
    first = near_bound(n)
    for c in range(chunks):
        besides[c][...] = neighbours[c][fetch_ref[index ^ 1]]
    for k in range(1, n // 2):
        mine, other = lists[k][index], lists[k][index ^ 1]
        for c in range(chunks):
            if k < first:
                out, at = outs[k - 1], 2 * c
            else:
                out, at = outs[first - 1 + c * (n // 2 - first) + k - first], 0
            out[at] = tabs[c][mine]
            out[at + 1] = neighbours[c][other]
    for k, one in enumerate(lists):
        for j in range(n):
            asked_ref[k, j] = one[j]


def pick(me, fetch, lists, tabs, neighbours):
    n = fetch.shape[0]
    chunks = len(tabs)
    first = near_bound(n)
    tile, dtype = tabs[0].shape[1:], tabs[0].dtype
    near, far = first - 1, n // 2 - first
    outs = pl.pallas_call(
        functools.partial(pick_kernel, chunks),
        out_shape=[sds((n // 2, n), fetch.dtype)]
        + [held(tile, dtype)] * chunks
        + [held((2 * chunks,) + tile, dtype)] * near
        + [held((2,) + tile, dtype)] * (chunks * far),
        in_specs=[SMEM] * (2 + len(lists)) + [VMEM] * (2 * chunks),
        out_specs=[SMEM] + [VMEM] * (chunks + near + chunks * far),
        compiler_params=PARAMS,
        name="pick",
    )(me, fetch, *lists[::-1], *tabs, *neighbours)
    far_parts = outs[1 + chunks + near :]
    return (
        outs[0],
        outs[1 : 1 + chunks],
        outs[1 + chunks : 1 + chunks + near],
        [far_parts[c * far : (c + 1) * far] for c in range(chunks)],
    )


def after(value, *others):
    return lax.optimization_barrier((value, others))[0]


def swap(value, n):
    return lax.ppermute(value, "rows", [(i, i ^ 1) for i in range(n)])


def send(parts, ks, n):
    return [
        lax.ppermute(part, "rows", [(i, i ^ (2 * k)) for i in range(n)])
        for part, k in zip(parts, ks)
    ]


def run_list(which, items_ref, blocks, rhs, totals, ready=None):
    first, groups = which
    own = totals[0].shape[0] - 1
    low, high = (1 << B_SHIFT) - 1, (1 << (T_SHIFT - B_SHIFT)) - 1

    def step(g, waited):
        at = first + g * GROUP
        if ready is not None:
            last = jnp.minimum(items_ref[at + GROUP - 1] >> T_SHIFT, own - 1) + 1
            lax.fori_loop(waited, last, ready, 0)
            waited = jnp.maximum(waited, last)
        for i in range(GROUP):
            word = items_ref[at + i]
            t = word >> T_SHIFT
            value = jnp.dot(
                blocks[(word >> B_SHIFT) & high],
                rhs(word & low),
                preferred_element_type=jnp.float32,
            )
            for c, total in enumerate(totals):
                total[t] += value[:, c * LANES : (c + 1) * LANES]
        return waited

    waited = lax.fori_loop(0, groups, step, jnp.int32(0))
    if ready is not None:
        lax.fori_loop(waited, own, ready, 0)


def column(ref, t, tile_rows):
    parts = tile_rows // LANES
    rows = [ref[pl.ds(t * parts + i, 1), :] for i in range(parts)]
    return jnp.concatenate(
        [jnp.broadcast_to(row, (LANES, LANES)).T for row in rows], axis=0
    )


def start_totals(me_ref, seeds_ref, totals):
    own, tile_rows = totals[0].shape[0] - 1, totals[0].shape[1]
    share = (1.0 - blend) / blend
    lane = lax.broadcasted_iota(jnp.int32, totals[0].shape[1:], 1)
    for t in range(own):
        seeds = column(seeds_ref, t, tile_rows) - me_ref[1]
        for c, total in enumerate(totals):
            total[t] = jnp.where(seeds == lane + c * LANES, share, 0.0)


def side_by_side(tabs):
    return lambda f: jnp.concatenate([tab[f] for tab in tabs], axis=1)


def prepare_kernel(room, me_ref, links_ref, counts_ref, fetch_ref, items_ref, sizes_ref):
    fill_lists(room, me_ref[0], links_ref, counts_ref, fetch_ref, items_ref, sizes_ref)


def prepare(me, links, counts, fetch):
    room = links.size + GROUP
    return pl.pallas_call(
        functools.partial(prepare_kernel, room),
        out_shape=[sds((3 * room,), jnp.int32), sds((4,), jnp.int32)],
        in_specs=[SMEM] * 4,
        out_specs=[SMEM] * 2,
        compiler_params=PARAMS,
        cost_estimate=COST,
        name="prepare",
    )(me, links, counts, fetch)


def begin_kernel(
    room, me_ref, items_ref, sizes_ref, counts_ref, blocks_hbm, prior, seeds_ref, blocks, *refs
):
    *totals, stage, tab, sems, prior_sem = refs
    own, groups = sems.shape
    slots = blocks.shape[0] // own
    size = slots // groups
    load = pltpu.make_async_copy(prior, stage, prior_sem)
    load.start()

    def copy(t, g):
        span = pl.ds(t * slots + g * size, size)
        return pltpu.make_async_copy(blocks_hbm.at[span], blocks.at[span], sems.at[t, g])

    def used(t):
        return (counts_ref[t] + size - 1) // size

    def begin(t, carry):
        return lax.fori_loop(0, used(t), lambda g, c: (copy(t, g).start(), c)[1], carry)

    def ready(t, carry):
        return lax.fori_loop(0, used(t), lambda g, c: (copy(t, g).wait(), c)[1], carry)

    lax.fori_loop(0, own, begin, 0)
    start_totals(me_ref, seeds_ref, totals)
    load.wait()
    for c in range(len(totals)):
        put_chunk(tab.at[:, :, pl.ds(c * LANES, LANES)], stage[...], c)
    run_list(own_list(room, sizes_ref), items_ref, blocks, lambda f: tab[f], totals, ready)


def begin(me, items, sizes, counts, blocks, prior, seeds, chunks):
    own, tile_rows = prior.shape[:2]
    slots = blocks.shape[0] // own
    size = next(g for g in (4, 3, 2, 1) if slots % g == 0)
    out = pl.pallas_call(
        functools.partial(begin_kernel, items.shape[0] // 3),
        out_shape=[held(blocks.shape, blocks.dtype)]
        + [held((own + 1, tile_rows, LANES), jnp.float32)] * chunks,
        in_specs=[SMEM] * 4 + [HBM] * 2 + [VMEM],
        out_specs=[VMEM] * (1 + chunks),
        scratch_shapes=[
            pltpu.VMEM(prior.shape, prior.dtype),
            pltpu.VMEM((own, tile_rows, chunks * LANES), prior.dtype),
            pltpu.SemaphoreType.DMA((own, slots // size)),
            pltpu.SemaphoreType.DMA,
        ],
        compiler_params=PARAMS,
        cost_estimate=COST,
        name="begin",
    )(me, items, sizes, counts, blocks, prior, seeds)
    return out[0], out[1:]


def own_kernel(chunks, room, me_ref, items_ref, sizes_ref, blocks, seeds_ref, temp_ref, *refs):
    tabs, wide_ref, totals = refs[:chunks], refs[chunks], refs[chunks + 1 :]
    start_totals(me_ref, seeds_ref, totals)
    own, tile_rows = wide_ref.shape[:2]
    for t in range(own):
        wide_ref[t] = blend * column(temp_ref, t, tile_rows)
    run_list(own_list(room, sizes_ref), items_ref, blocks, side_by_side(tabs), totals)


def own_part(me, items, sizes, blocks, seeds, temp, tabs):
    own, tile_rows = tabs[0].shape[:2]
    chunks = len(tabs)
    out = pl.pallas_call(
        functools.partial(own_kernel, chunks, items.shape[0] // 3),
        out_shape=[held((own, tile_rows, LANES), jnp.float32)]
        + [held((own + 1, tile_rows, LANES), jnp.float32)] * chunks,
        in_specs=[SMEM] * 3 + [VMEM] * (3 + chunks),
        out_specs=[VMEM] * (1 + chunks),
        compiler_params=PARAMS,
        cost_estimate=COST,
        name="own_part",
    )(me, items, sizes, blocks, seeds, temp, *tabs)
    return out[0], out[1:]


def put_near(chunk, near, field):
    for k, one in enumerate(near):
        for j in range(2):
            field[2 * (k + 1) + j] = one[2 * chunk + j]


def put_far(first, far, field):
    for k, one in enumerate(far):
        for j in range(2):
            field[2 * (first + k) + j] = one[j]


def put_pairs(first, arrived, got, field):
    for i, (one, other) in enumerate(zip(arrived, got)):
        field[2 * (first + i)] = one[0]
        field[2 * (first + i) + 1] = other[0]


def step1_kernel(
    nears, fars, chunk, room, me_ref, items_ref, sizes_ref, asked_ref, beside_ref, blocks, *refs
):
    tile, near, far = refs[0], refs[1 : 1 + nears], refs[1 + nears : 1 + nears + fars]
    begun, out, beside_tile, *messages, field, total = refs[1 + nears + fars :]
    own = out.shape[0]
    field[1] = tile[...]
    put_near(chunk, near, field)
    put_far(nears + 1, far, field)
    total[...] = begun[...]
    run_list(both_lists(room, sizes_ref), items_ref, blocks, lambda f: field[f], [total])
    for t in range(own):
        out[t] = (blend * total[t]).astype(out.dtype)
    index = me_ref[0]
    beside_tile[0] = out[beside_ref[0, index]]
    for k, message in enumerate(messages):
        message[0] = out[asked_ref[k + 1, index]]
        message[1] = out[beside_ref[k + 1, index]]


def step1(chunk, me, items, sizes, asked, beside, blocks, tile, near, far, begun):
    own, tile_rows = begun.shape[0] - 1, begun.shape[1]
    n = asked.shape[1]
    dtype = tile.dtype
    count = n // 2 - 1
    out = pl.pallas_call(
        functools.partial(step1_kernel, len(near), len(far), chunk, items.shape[0] // 3),
        out_shape=[
            held((own, tile_rows, LANES), dtype),
            held((1, tile_rows, LANES), dtype),
        ]
        + [held((2, tile_rows, LANES), dtype)] * count,
        in_specs=[SMEM] * 5 + [VMEM] * (3 + len(near) + len(far)),
        out_specs=[VMEM] * (2 + count),
        scratch_shapes=[
            pltpu.VMEM((n, tile_rows, LANES), dtype),
            pltpu.VMEM(begun.shape, begun.dtype),
        ],
        compiler_params=PARAMS,
        cost_estimate=COST,
        name="step1",
    )(me, items, sizes, asked, beside, blocks, tile, *near, *far, begun)
    return out[0], out[1], out[2:]


def near_kernel(nears, room, items_ref, sizes_ref, blocks, *refs):
    got, near, (_, total, field) = refs[: nears + 1], refs[nears + 1 : -3], refs[-3:]
    field[1] = got[0][0]
    put_pairs(1, near, got[1:], field)
    run_list(near_list(room, sizes_ref), items_ref, blocks, lambda f: field[f], [total])


def near_part(items, sizes, blocks, got, near, begun):
    tile_rows = begun.shape[1]
    return pl.pallas_call(
        functools.partial(near_kernel, len(near), items.shape[0] // 3),
        out_shape=held(begun.shape, begun.dtype),
        in_specs=[SMEM] * 2 + [VMEM] * (3 + 2 * len(near)),
        out_specs=VMEM,
        input_output_aliases={4 + 2 * len(near): 0},
        scratch_shapes=[pltpu.VMEM((2 * (len(near) + 1), tile_rows, LANES), got[0].dtype)],
        compiler_params=PARAMS,
        cost_estimate=COST,
        name="near_part",
    )(items, sizes, blocks, *got, *near, begun)


def row_sums(value):
    ones = jnp.ones((8, value.shape[1]), jnp.bfloat16)
    high = value.astype(jnp.bfloat16)
    low = (value - high.astype(jnp.float32)).astype(jnp.bfloat16)
    add = lambda part: lax.dot_general(
        ones, part, (((1,), (1,)), ((), ())), preferred_element_type=jnp.float32
    )
    return add(high) + add(low)


def step2_kernel(gots, count, live, whole, room, items_ref, sizes_ref, blocks, *refs):
    got, arrived = refs[:gots], refs[gots : gots + count]
    begun, wide_ref = refs[gots + count : gots + count + 2]
    *earlier, expo_ref, stats_ref, field, total = refs[gots + count + 2 :]
    own, tile_rows = expo_ref.shape[:2]
    if whole:
        field[1] = got[0][0]
        put_far(1, arrived, field)
    else:
        put_pairs(field.shape[0] // 2 - count, arrived, got, field)
    total[...] = begun[...]
    which = (both_lists if whole else far_list)(room, sizes_ref)
    run_list(which, items_ref, blocks, lambda f: field[f], [total])
    parts = tile_rows // LANES
    last = stats_ref.shape[0] - 1
    if earlier:
        stats_ref[:last] = earlier[0][...]
    for t in range(own):
        logits = wide_ref[t] * total[t]
        lane = lax.broadcasted_iota(jnp.int32, logits.shape, 1)
        if live < LANES:
            top = jnp.max(jnp.where(lane < live, logits, -jnp.inf), axis=1, keepdims=True)
            shifted = jnp.where(lane < live, logits - top, 0.0)
            expo = jnp.where(lane < live, jnp.exp(shifted), 0.0)
        else:
            top = jnp.max(logits, axis=1, keepdims=True)
            shifted = logits - top
            expo = jnp.exp(shifted)
        expo_ref[t] = expo
        sums, moments = row_sums(expo), row_sums(expo * shifted)
        for i in range(parts):
            span, at = slice(i * LANES, (i + 1) * LANES), slice(t * parts + i, t * parts + i + 1)
            flat = jnp.broadcast_to(top[span], (LANES, LANES)).T
            stats_ref[last, 0, at, :] = flat[:1]
            stats_ref[last, 1, at, :] = sums[:1, span]
            stats_ref[last, 2, at, :] = moments[:1, span]


def step2(live, whole, n, items, sizes, blocks, got, arrived, begun, wide, earlier):
    own, tile_rows = begun.shape[0] - 1, begun.shape[1]
    before = () if earlier is None else (earlier,)
    count = 1 + (earlier.shape[0] if before else 0)
    return pl.pallas_call(
        functools.partial(
            step2_kernel, len(got), len(arrived), live, whole, items.shape[0] // 3
        ),
        out_shape=[
            held((own, tile_rows, LANES), jnp.float32),
            held((count, 3, own * tile_rows // LANES, LANES), jnp.float32),
        ],
        in_specs=[SMEM] * 2 + [VMEM] * (3 + len(got) + len(arrived) + len(before)),
        out_specs=[VMEM] * 2,
        scratch_shapes=[
            pltpu.VMEM((n, tile_rows, LANES), got[0].dtype),
            pltpu.VMEM(begun.shape, begun.dtype),
        ],
        compiler_params=PARAMS,
        cost_estimate=COST,
        name="step2",
    )(items, sizes, blocks, *got, *arrived, begun, wide, *before)


def finish_kernel(chunks, parts, *refs):
    expos, stats = refs[:chunks], refs[chunks : chunks + parts]
    pseudo_ref, certainty_ref, scale_ref = refs[chunks + parts :]
    own, tile_rows = expos[0].shape[:2]
    width = pseudo_ref.shape[1]
    every = [(s, c) for s in stats for c in range(chunks)]
    top = functools.reduce(jnp.maximum, [s[c, 0] for s, c in every])
    totals, moments, scales = 0.0, 0.0, []
    for s, c in every:
        delta = s[c, 0] - top
        scale = jnp.exp(delta)
        scales.append(scale)
        totals += scale * s[c, 1]
        moments += scale * (s[c, 2] + delta * s[c, 1])
    certainty_ref[...] = 1.0 - (jnp.log(totals) - moments / totals) / jnp.log(jnp.float32(CLS))
    inverse = 1.0 / totals
    for c in range(chunks):
        scale_ref[c] = scales[c] * inverse
    for t in range(own):
        span = slice(t * tile_rows, (t + 1) * tile_rows)
        for c in range(chunks):
            start = c * LANES
            live = min(LANES, width - start)
            value = expos[c][t] * column(scale_ref.at[c], t, tile_rows)
            pseudo_ref[span, start : start + live] = value[:, :live].astype(pseudo_ref.dtype)


def finish(expos, stats, width):
    own, tile_rows = expos[0].shape[:2]
    rows = own * tile_rows
    chunks, parts = len(expos), len(stats)
    return pl.pallas_call(
        functools.partial(finish_kernel, chunks, parts),
        out_shape=[sds((rows, width), jnp.bfloat16), sds((rows // LANES, LANES), jnp.float32)],
        in_specs=[VMEM] * (chunks + parts),
        out_specs=[VMEM] * 2,
        scratch_shapes=[pltpu.VMEM((chunks, rows // LANES, LANES), jnp.float32)],
        compiler_params=PARAMS,
        name="finish",
    )(*expos, *stats)


def local(prior, blocks, links, counts, fetch, seeds, inv_temp):
    width = prior.shape[1]
    tile_rows = blocks.shape[2]
    n = lax.axis_size("rows")
    parts = lax.axis_size("cls")
    chunks = pl.cdiv(width, LANES)
    me = jnp.stack([lax.axis_index("rows"), lax.axis_index("cls") * width]).astype(jnp.int32)
    fetch = fetch.reshape(n)
    first = near_bound(n)
    near_ks, far_ks = range(1, first), range(first, n // 2)
    neighbour = swap(prior, n).reshape(-1, tile_rows, width)
    prior = prior.reshape(-1, tile_rows, width)
    lists = send([fetch] * (n // 2 - 1), range(1, n // 2), n)
    tabs, neighbours = split(prior, chunks), split(neighbour, chunks)
    blocks = blocks.reshape((-1,) + blocks.shape[2:])
    seeds = seeds.reshape(-1, LANES)
    temp = inv_temp.reshape(-1, LANES)

    asked, tiles, near_sent, far_sent = pick(me, fetch, lists, tabs, neighbours)
    beside = swap(asked, n)
    near = send(near_sent, near_ks, n)
    far = [send(far_sent[0], far_ks, n)]
    items, sizes = prepare(me, links, counts, after(fetch, near_sent, far_sent))
    parcels = []
    for c in range(1, chunks):
        parcels = [after(part, sizes, beside) for part in far_sent[c]]
        far.append(send(parcels, far_ks, n))
    blocks, begun = begin(
        me, items, sizes, counts, after(blocks, parcels), prior, seeds, chunks
    )
    firsts, there = [], []
    ks = range(1, n // 2)
    for c in range(chunks):
        out, tile, parcels = step1(
            c, me, items, sizes, asked, beside, blocks, tiles[c], near, far[c],
            after(begun[c], parcels),
        )
        firsts.append(out)
        if c < chunks - 1:
            seconds = [swap(part[1:], n) for part in parcels]
            parcels = [jnp.concatenate([p[:1], q]) for p, q in zip(parcels, seconds)]
        elif there:
            parcels = [after(part, there[-1][1][: first - 1]) for part in parcels]
        if c < chunks - 1:
            parcels = [after(p, parcels[first - 1 :]) for p in parcels[: first - 1]] + parcels[first - 1 :]
        there.append((tile, send(parcels[::-1], ks[::-1], n)[::-1]))
    wide, begun = own_part(me, items, sizes, blocks, after(seeds, parcels), temp, firsts)
    expos, stats = [], None
    for c in range(chunks):
        live = min(LANES, width - c * LANES)
        (tile, here), total = there[c], begun[c]
        if c < chunks - 1:
            got = [swap(after(tile, begun), n)]
        else:
            near, here = here[: first - 1], here[first - 1 :]
            tile = after(tile, near)
            got = [swap(part, n) for part in [tile] + [part[1:] for part in near]]
            total = near_part(items, sizes, blocks, got, near, total)
            if stats is not None:
                here = [after(part, stats) for part in here]
            got = [swap(part[1:], n) for part in here]
        expo, stats = step2(
            live, c < chunks - 1, n, items, sizes, blocks, got, here, total, wide, stats
        )
        expos.append(expo)
    stats = [stats] + [
        lax.ppermute(stats, "cls", [(i, (i + k) % parts) for i in range(parts)])
        for k in range(1, parts)
    ]
    pseudo, certainty = finish(expos, stats, width)
    return pseudo, certainty.reshape(-1)


def solution(mesh):
    return jax.shard_map(
        local,
        mesh=mesh,
        in_specs=(
            P("rows", "cls"),
            P("rows", None, None, None),
            P("rows", None),
            P("rows"),
            P("rows", None, None),
            P("rows"),
            P("rows"),
        ),
        out_specs=(P("rows", "cls"), P("rows")),
        check_vma=False,
    )
```

```python
import functools

import jax
import jax.numpy as jnp
from jax import lax
from jax.experimental import pallas as pl
from jax.experimental.pallas import tpu as pltpu
from jax.sharding import PartitionSpec as P

CLS = 1000
LANES = 128
GROUP = 16
blend = 0.8

SMEM = pl.BlockSpec(memory_space=pltpu.SMEM)
VMEM = pl.BlockSpec(memory_space=pltpu.VMEM)
HBM = pl.BlockSpec(memory_space=pltpu.HBM)
T_SHIFT, B_SHIFT = 20, 8


COST = pl.CostEstimate(flops=1, bytes_accessed=1, transcendentals=0)


PARAMS = pltpu.CompilerParams(vmem_limit_bytes=8 << 20)


def held(shape, dtype):
    return pltpu.VMEM(shape, dtype)


def sds(shape, dtype):
    return jax.ShapeDtypeStruct(shape, dtype)


def put_chunk(out, value, chunk):
    start = chunk * LANES
    live = min(LANES, value.shape[-1] - start)
    out[..., :live] = value[..., start : start + live]
    if live < LANES:
        out[..., live:] = jnp.zeros(value.shape[:-1] + (LANES - live,), out.dtype)


def fill_lists(room, index, links_ref, counts_ref, fetch_ref, items_ref, sizes_ref):
    own, slots = links_ref.shape
    n = fetch_ref.shape[0]
    mine = fetch_ref[index]

    def tile(t, sizes):
        def slot(j, sizes):
            v = links_ref[t, j]
            x = (v - own) ^ index
            is_own = jnp.logical_or(v < own, x == 0)
            is_near = jnp.logical_and(jnp.logical_not(is_own), x < n // 2)
            field = jnp.where(is_own, jnp.where(v < own, v, mine), x)
            place = jnp.where(
                is_own, sizes[0], jnp.where(is_near, 2 * room + sizes[1], 2 * room - 1 - sizes[2])
            )
            items_ref[place] = (t << T_SHIFT) + ((t * slots + j) << B_SHIFT) + field
            is_far = jnp.logical_not(jnp.logical_or(is_own, is_near))
            return tuple(
                size + kind.astype(jnp.int32) for size, kind in zip(sizes, (is_own, is_near, is_far))
            )

        return lax.fori_loop(0, counts_ref[t], slot, sizes)

    sizes = lax.fori_loop(0, own, tile, (jnp.int32(0),) * 3)
    for kind in range(3):
        sizes_ref[kind] = sizes[kind]
    sizes_ref[3] = fetch_ref[index ^ 1]

    def fill(i, carry):
        items_ref[sizes[0] + i] = own << T_SHIFT
        items_ref[2 * room + sizes[1] + i] = own << T_SHIFT
        items_ref[2 * room - sizes[2] - 1 - i] = own << T_SHIFT
        return carry

    lax.fori_loop(0, GROUP, fill, 0)


def groups_of(count):
    return (count + GROUP - 1) // GROUP


def own_list(room, sizes_ref):
    return 0, groups_of(sizes_ref[0])


def near_list(room, sizes_ref):
    return 2 * room, groups_of(sizes_ref[1])


def far_list(room, sizes_ref):
    groups = groups_of(sizes_ref[2])
    return 2 * room - groups * GROUP, groups


def both_lists(room, sizes_ref):
    return 2 * room - sizes_ref[2], groups_of(sizes_ref[1] + sizes_ref[2])


def near_bound(n):
    return max(1, n // 4)


def split_kernel(prior_ref, *outs):
    for c, out in enumerate(outs):
        put_chunk(out, prior_ref[...], c)


def split(prior, chunks):
    return pl.pallas_call(
        split_kernel,
        out_shape=[held(prior.shape[:2] + (LANES,), prior.dtype)] * chunks,
        in_specs=[VMEM],
        out_specs=[VMEM] * chunks,
        compiler_params=PARAMS,
        name="split",
    )(prior)


def pick_kernel(chunks, me_ref, fetch_ref, *refs):
    n = fetch_ref.shape[0]
    count = n // 2 - 1
    lists = (fetch_ref,) + refs[:count][::-1]
    tabs, neighbours = refs[count : count + chunks], refs[count + chunks : count + 2 * chunks]
    asked_ref, *outs = refs[count + 2 * chunks :]
    besides, outs = outs[:chunks], outs[chunks:]
    index = me_ref[0]
    first = near_bound(n)
    for c in range(chunks):
        besides[c][...] = neighbours[c][fetch_ref[index ^ 1]]
    for k in range(1, n // 2):
        mine, other = lists[k][index], lists[k][index ^ 1]
        for c in range(chunks):
            if k < first:
                out, at = outs[k - 1], 2 * c
            else:
                out, at = outs[first - 1 + c * (n // 2 - first) + k - first], 0
            out[at] = tabs[c][mine]
            out[at + 1] = neighbours[c][other]
    for k, one in enumerate(lists):
        for j in range(n):
            asked_ref[k, j] = one[j]


def pick(me, fetch, lists, tabs, neighbours):
    n = fetch.shape[0]
    chunks = len(tabs)
    first = near_bound(n)
    tile, dtype = tabs[0].shape[1:], tabs[0].dtype
    near, far = first - 1, n // 2 - first
    outs = pl.pallas_call(
        functools.partial(pick_kernel, chunks),
        out_shape=[sds((n // 2, n), fetch.dtype)]
        + [held(tile, dtype)] * chunks
        + [held((2 * chunks,) + tile, dtype)] * near
        + [held((2,) + tile, dtype)] * (chunks * far),
        in_specs=[SMEM] * (2 + len(lists)) + [VMEM] * (2 * chunks),
        out_specs=[SMEM] + [VMEM] * (chunks + near + chunks * far),
        compiler_params=PARAMS,
        name="pick",
    )(me, fetch, *lists[::-1], *tabs, *neighbours)
    far_parts = outs[1 + chunks + near :]
    return (
        outs[0],
        outs[1 : 1 + chunks],
        outs[1 + chunks : 1 + chunks + near],
        [far_parts[c * far : (c + 1) * far] for c in range(chunks)],
    )


def after(value, *others):
    return lax.optimization_barrier((value, others))[0]


def swap(value, n):
    return lax.ppermute(value, "rows", [(i, i ^ 1) for i in range(n)])


def send(parts, ks, n):
    return [
        lax.ppermute(part, "rows", [(i, i ^ (2 * k)) for i in range(n)])
        for part, k in zip(parts, ks)
    ]


def run_list(which, items_ref, blocks, rhs, totals, ready=None):
    first, groups = which
    own = totals[0].shape[0] - 1
    low, high = (1 << B_SHIFT) - 1, (1 << (T_SHIFT - B_SHIFT)) - 1

    def step(g, waited):
        at = first + g * GROUP
        if ready is not None:
            last = jnp.minimum(items_ref[at + GROUP - 1] >> T_SHIFT, own - 1) + 1
            lax.fori_loop(waited, last, ready, 0)
            waited = jnp.maximum(waited, last)
        for i in range(GROUP):
            word = items_ref[at + i]
            t = word >> T_SHIFT
            value = jnp.dot(
                blocks[(word >> B_SHIFT) & high],
                rhs(word & low),
                preferred_element_type=jnp.float32,
            )
            for c, total in enumerate(totals):
                total[t] += value[:, c * LANES : (c + 1) * LANES]
        return waited

    waited = lax.fori_loop(0, groups, step, jnp.int32(0))
    if ready is not None:
        lax.fori_loop(waited, own, ready, 0)


def column(ref, t, tile_rows):
    parts = tile_rows // LANES
    rows = [ref[pl.ds(t * parts + i, 1), :] for i in range(parts)]
    return jnp.concatenate(
        [jnp.broadcast_to(row, (LANES, LANES)).T for row in rows], axis=0
    )


def start_totals(me_ref, seeds_ref, totals):
    own, tile_rows = totals[0].shape[0] - 1, totals[0].shape[1]
    share = (1.0 - blend) / blend
    lane = lax.broadcasted_iota(jnp.int32, totals[0].shape[1:], 1)
    for t in range(own):
        seeds = column(seeds_ref, t, tile_rows) - me_ref[1]
        for c, total in enumerate(totals):
            total[t] = jnp.where(seeds == lane + c * LANES, share, 0.0)


def side_by_side(tabs):
    return lambda f: jnp.concatenate([tab[f] for tab in tabs], axis=1)


def prepare_kernel(room, me_ref, links_ref, counts_ref, fetch_ref, items_ref, sizes_ref):
    fill_lists(room, me_ref[0], links_ref, counts_ref, fetch_ref, items_ref, sizes_ref)


def prepare(me, links, counts, fetch):
    room = links.size + GROUP
    return pl.pallas_call(
        functools.partial(prepare_kernel, room),
        out_shape=[sds((3 * room,), jnp.int32), sds((4,), jnp.int32)],
        in_specs=[SMEM] * 4,
        out_specs=[SMEM] * 2,
        compiler_params=PARAMS,
        cost_estimate=COST,
        name="prepare",
    )(me, links, counts, fetch)


def begin_kernel(
    room, me_ref, items_ref, sizes_ref, counts_ref, blocks_hbm, prior, seeds_ref, blocks, *refs
):
    *totals, stage, tab, sems, prior_sem = refs
    own, groups = sems.shape
    slots = blocks.shape[0] // own
    size = slots // groups
    load = pltpu.make_async_copy(prior, stage, prior_sem)
    load.start()

    def copy(t, g):
        span = pl.ds(t * slots + g * size, size)
        return pltpu.make_async_copy(blocks_hbm.at[span], blocks.at[span], sems.at[t, g])

    def used(t):
        return (counts_ref[t] + size - 1) // size

    def begin(t, carry):
        return lax.fori_loop(0, used(t), lambda g, c: (copy(t, g).start(), c)[1], carry)

    def ready(t, carry):
        return lax.fori_loop(0, used(t), lambda g, c: (copy(t, g).wait(), c)[1], carry)

    lax.fori_loop(0, own, begin, 0)
    start_totals(me_ref, seeds_ref, totals)
    load.wait()
    for c in range(len(totals)):
        put_chunk(tab.at[:, :, pl.ds(c * LANES, LANES)], stage[...], c)
    run_list(own_list(room, sizes_ref), items_ref, blocks, lambda f: tab[f], totals, ready)


def begin(me, items, sizes, counts, blocks, prior, seeds, chunks):
    own, tile_rows = prior.shape[:2]
    slots = blocks.shape[0] // own
    size = next(g for g in (4, 3, 2, 1) if slots % g == 0)
    out = pl.pallas_call(
        functools.partial(begin_kernel, items.shape[0] // 3),
        out_shape=[held(blocks.shape, blocks.dtype)]
        + [held((own + 1, tile_rows, LANES), jnp.float32)] * chunks,
        in_specs=[SMEM] * 4 + [HBM] * 2 + [VMEM],
        out_specs=[VMEM] * (1 + chunks),
        scratch_shapes=[
            pltpu.VMEM(prior.shape, prior.dtype),
            pltpu.VMEM((own, tile_rows, chunks * LANES), prior.dtype),
            pltpu.SemaphoreType.DMA((own, slots // size)),
            pltpu.SemaphoreType.DMA,
        ],
        compiler_params=PARAMS,
        cost_estimate=COST,
        name="begin",
    )(me, items, sizes, counts, blocks, prior, seeds)
    return out[0], out[1:]


def own_kernel(chunks, room, me_ref, items_ref, sizes_ref, blocks, seeds_ref, temp_ref, *refs):
    tabs, wide_ref, totals = refs[:chunks], refs[chunks], refs[chunks + 1 :]
    start_totals(me_ref, seeds_ref, totals)
    own, tile_rows = wide_ref.shape[:2]
    for t in range(own):
        wide_ref[t] = blend * column(temp_ref, t, tile_rows)
    run_list(own_list(room, sizes_ref), items_ref, blocks, side_by_side(tabs), totals)


def own_part(me, items, sizes, blocks, seeds, temp, tabs):
    own, tile_rows = tabs[0].shape[:2]
    chunks = len(tabs)
    out = pl.pallas_call(
        functools.partial(own_kernel, chunks, items.shape[0] // 3),
        out_shape=[held((own, tile_rows, LANES), jnp.float32)]
        + [held((own + 1, tile_rows, LANES), jnp.float32)] * chunks,
        in_specs=[SMEM] * 3 + [VMEM] * (3 + chunks),
        out_specs=[VMEM] * (1 + chunks),
        compiler_params=PARAMS,
        cost_estimate=COST,
        name="own_part",
    )(me, items, sizes, blocks, seeds, temp, *tabs)
    return out[0], out[1:]


def put_near(chunk, near, field):
    for k, one in enumerate(near):
        for j in range(2):
            field[2 * (k + 1) + j] = one[2 * chunk + j]


def put_far(first, far, field):
    for k, one in enumerate(far):
        for j in range(2):
            field[2 * (first + k) + j] = one[j]


def put_pairs(first, arrived, got, field):
    for i, (one, other) in enumerate(zip(arrived, got)):
        field[2 * (first + i)] = one[0]
        field[2 * (first + i) + 1] = other[0]


def step1_kernel(
    nears, fars, chunk, room, me_ref, items_ref, sizes_ref, asked_ref, beside_ref, blocks, *refs
):
    tile, near, far = refs[0], refs[1 : 1 + nears], refs[1 + nears : 1 + nears + fars]
    _, total, out, beside_tile, *messages, field = refs[1 + nears + fars :]
    own = out.shape[0]
    field[1] = tile[...]
    put_near(chunk, near, field)
    put_far(nears + 1, far, field)
    run_list(both_lists(room, sizes_ref), items_ref, blocks, lambda f: field[f], [total])
    for t in range(own):
        out[t] = (blend * total[t]).astype(out.dtype)
    index = me_ref[0]
    beside_tile[0] = out[beside_ref[0, index]]
    for k, message in enumerate(messages):
        message[0] = out[asked_ref[k + 1, index]]
        message[1] = out[beside_ref[k + 1, index]]


def step1(chunk, me, items, sizes, asked, beside, blocks, tile, near, far, begun):
    own, tile_rows = begun.shape[0] - 1, begun.shape[1]
    n = asked.shape[1]
    dtype = tile.dtype
    count = n // 2 - 1
    out = pl.pallas_call(
        functools.partial(step1_kernel, len(near), len(far), chunk, items.shape[0] // 3),
        out_shape=[
            held(begun.shape, begun.dtype),
            held((own, tile_rows, LANES), dtype),
            held((1, tile_rows, LANES), dtype),
        ]
        + [held((2, tile_rows, LANES), dtype)] * count,
        in_specs=[SMEM] * 5 + [VMEM] * (3 + len(near) + len(far)),
        out_specs=[VMEM] * (3 + count),
        input_output_aliases={7 + len(near) + len(far): 0},
        scratch_shapes=[pltpu.VMEM((n, tile_rows, LANES), dtype)],
        compiler_params=PARAMS,
        cost_estimate=COST,
        name="step1",
    )(me, items, sizes, asked, beside, blocks, tile, *near, *far, begun)
    return out[1], out[2], out[3:]


def near_kernel(nears, room, items_ref, sizes_ref, blocks, *refs):
    got, near, (_, total, field) = refs[: nears + 1], refs[nears + 1 : -3], refs[-3:]
    field[1] = got[0][0]
    put_pairs(1, near, got[1:], field)
    run_list(near_list(room, sizes_ref), items_ref, blocks, lambda f: field[f], [total])


def near_part(items, sizes, blocks, got, near, begun):
    tile_rows = begun.shape[1]
    return pl.pallas_call(
        functools.partial(near_kernel, len(near), items.shape[0] // 3),
        out_shape=held(begun.shape, begun.dtype),
        in_specs=[SMEM] * 2 + [VMEM] * (3 + 2 * len(near)),
        out_specs=VMEM,
        input_output_aliases={4 + 2 * len(near): 0},
        scratch_shapes=[pltpu.VMEM((2 * (len(near) + 1), tile_rows, LANES), got[0].dtype)],
        compiler_params=PARAMS,
        cost_estimate=COST,
        name="near_part",
    )(items, sizes, blocks, *got, *near, begun)


def row_sums(value):
    ones = jnp.ones((8, value.shape[1]), jnp.bfloat16)
    high = value.astype(jnp.bfloat16)
    low = (value - high.astype(jnp.float32)).astype(jnp.bfloat16)
    add = lambda part: lax.dot_general(
        ones, part, (((1,), (1,)), ((), ())), preferred_element_type=jnp.float32
    )
    return add(high) + add(low)


def step2_kernel(gots, count, live, whole, room, items_ref, sizes_ref, blocks, *refs):
    got, arrived = refs[:gots], refs[gots : gots + count]
    _, wide_ref = refs[gots + count : gots + count + 2]
    *earlier, total, expo_ref, stats_ref, field = refs[gots + count + 2 :]
    own, tile_rows = expo_ref.shape[:2]
    if whole:
        field[1] = got[0][0]
        put_far(1, arrived, field)
    else:
        put_pairs(field.shape[0] // 2 - count, arrived, got, field)
    which = (both_lists if whole else far_list)(room, sizes_ref)
    run_list(which, items_ref, blocks, lambda f: field[f], [total])
    parts = tile_rows // LANES
    last = stats_ref.shape[0] - 1
    if earlier:
        stats_ref[:last] = earlier[0][...]
    for t in range(own):
        logits = wide_ref[t] * total[t]
        lane = lax.broadcasted_iota(jnp.int32, logits.shape, 1)
        if live < LANES:
            top = jnp.max(jnp.where(lane < live, logits, -jnp.inf), axis=1, keepdims=True)
            shifted = jnp.where(lane < live, logits - top, 0.0)
            expo = jnp.where(lane < live, jnp.exp(shifted), 0.0)
        else:
            top = jnp.max(logits, axis=1, keepdims=True)
            shifted = logits - top
            expo = jnp.exp(shifted)
        expo_ref[t] = expo
        sums, moments = row_sums(expo), row_sums(expo * shifted)
        for i in range(parts):
            span, at = slice(i * LANES, (i + 1) * LANES), slice(t * parts + i, t * parts + i + 1)
            flat = jnp.broadcast_to(top[span], (LANES, LANES)).T
            stats_ref[last, 0, at, :] = flat[:1]
            stats_ref[last, 1, at, :] = sums[:1, span]
            stats_ref[last, 2, at, :] = moments[:1, span]


def step2(live, whole, n, items, sizes, blocks, got, arrived, begun, wide, earlier):
    own, tile_rows = begun.shape[0] - 1, begun.shape[1]
    before = () if earlier is None else (earlier,)
    count = 1 + (earlier.shape[0] if before else 0)
    out = pl.pallas_call(
        functools.partial(
            step2_kernel, len(got), len(arrived), live, whole, items.shape[0] // 3
        ),
        out_shape=[
            held(begun.shape, begun.dtype),
            held((own, tile_rows, LANES), jnp.float32),
            held((count, 3, own * tile_rows // LANES, LANES), jnp.float32),
        ],
        in_specs=[SMEM] * 2 + [VMEM] * (3 + len(got) + len(arrived) + len(before)),
        out_specs=[VMEM] * 3,
        input_output_aliases={3 + len(got) + len(arrived): 0},
        scratch_shapes=[pltpu.VMEM((n, tile_rows, LANES), got[0].dtype)],
        compiler_params=PARAMS,
        cost_estimate=COST,
        name="step2",
    )(items, sizes, blocks, *got, *arrived, begun, wide, *before)
    return out[1:]


def finish_kernel(chunks, parts, *refs):
    expos, stats = refs[:chunks], refs[chunks : chunks + parts]
    pseudo_ref, certainty_ref, scale_ref = refs[chunks + parts :]
    own, tile_rows = expos[0].shape[:2]
    width = pseudo_ref.shape[1]
    every = [(s, c) for s in stats for c in range(chunks)]
    top = functools.reduce(jnp.maximum, [s[c, 0] for s, c in every])
    totals, moments, scales = 0.0, 0.0, []
    for s, c in every:
        delta = s[c, 0] - top
        scale = jnp.exp(delta)
        scales.append(scale)
        totals += scale * s[c, 1]
        moments += scale * (s[c, 2] + delta * s[c, 1])
    certainty_ref[...] = 1.0 - (jnp.log(totals) - moments / totals) / jnp.log(jnp.float32(CLS))
    inverse = 1.0 / totals
    for c in range(chunks):
        scale_ref[c] = scales[c] * inverse
    for t in range(own):
        span = slice(t * tile_rows, (t + 1) * tile_rows)
        for c in range(chunks):
            start = c * LANES
            live = min(LANES, width - start)
            value = expos[c][t] * column(scale_ref.at[c], t, tile_rows)
            pseudo_ref[span, start : start + live] = value[:, :live].astype(pseudo_ref.dtype)


def finish(expos, stats, width):
    own, tile_rows = expos[0].shape[:2]
    rows = own * tile_rows
    chunks, parts = len(expos), len(stats)
    return pl.pallas_call(
        functools.partial(finish_kernel, chunks, parts),
        out_shape=[sds((rows, width), jnp.bfloat16), sds((rows // LANES, LANES), jnp.float32)],
        in_specs=[VMEM] * (chunks + parts),
        out_specs=[VMEM] * 2,
        scratch_shapes=[pltpu.VMEM((chunks, rows // LANES, LANES), jnp.float32)],
        compiler_params=PARAMS,
        name="finish",
    )(*expos, *stats)


def local(prior, blocks, links, counts, fetch, seeds, inv_temp):
    width = prior.shape[1]
    tile_rows = blocks.shape[2]
    n = lax.axis_size("rows")
    parts = lax.axis_size("cls")
    chunks = pl.cdiv(width, LANES)
    me = jnp.stack([lax.axis_index("rows"), lax.axis_index("cls") * width]).astype(jnp.int32)
    fetch = fetch.reshape(n)
    first = near_bound(n)
    near_ks, far_ks = range(1, first), range(first, n // 2)
    neighbour = swap(prior, n).reshape(-1, tile_rows, width)
    prior = prior.reshape(-1, tile_rows, width)
    lists = send([fetch] * (n // 2 - 1), range(1, n // 2), n)
    tabs, neighbours = split(prior, chunks), split(neighbour, chunks)
    blocks = blocks.reshape((-1,) + blocks.shape[2:])
    seeds = seeds.reshape(-1, LANES)
    temp = inv_temp.reshape(-1, LANES)

    asked, tiles, near_sent, far_sent = pick(me, fetch, lists, tabs, neighbours)
    beside = swap(asked, n)
    near = send(near_sent, near_ks, n)
    far = [send(far_sent[0], far_ks, n)]
    items, sizes = prepare(me, links, counts, after(fetch, near_sent, far_sent))
    parcels = []
    for c in range(1, chunks):
        parcels = [after(part, sizes, beside) for part in far_sent[c]]
        far.append(send(parcels, far_ks, n))
    blocks, begun = begin(
        me, items, sizes, counts, after(blocks, parcels), prior, seeds, chunks
    )
    firsts, there = [], []
    ks = range(1, n // 2)
    for c in range(chunks):
        out, tile, parcels = step1(
            c, me, items, sizes, asked, beside, blocks, tiles[c], near, far[c],
            after(begun[c], parcels),
        )
        firsts.append(out)
        if c < chunks - 1:
            seconds = [swap(part[1:], n) for part in parcels]
            parcels = [jnp.concatenate([p[:1], q]) for p, q in zip(parcels, seconds)]
        elif there:
            parcels = [after(part, there[-1][1][: first - 1]) for part in parcels]
        if c < chunks - 1:
            parcels = [after(p, parcels[first - 1 :]) for p in parcels[: first - 1]] + parcels[first - 1 :]
        there.append((tile, send(parcels[::-1], ks[::-1], n)[::-1]))
    wide, begun = own_part(me, items, sizes, blocks, after(seeds, parcels), temp, firsts)
    expos, stats = [], None
    for c in range(chunks):
        live = min(LANES, width - c * LANES)
        (tile, here), total = there[c], begun[c]
        if c < chunks - 1:
            got = [swap(after(tile, begun), n)]
        else:
            near, here = here[: first - 1], here[first - 1 :]
            tile = after(tile, near)
            got = [swap(part, n) for part in [tile] + [part[1:] for part in near]]
            total = near_part(items, sizes, blocks, got, near, total)
            if stats is not None:
                here = [after(part, stats) for part in here]
            got = [swap(part[1:], n) for part in here]
        expo, stats = step2(
            live, c < chunks - 1, n, items, sizes, blocks, got, here, total, wide, stats
        )
        expos.append(expo)
    stats = [stats] + [
        lax.ppermute(stats, "cls", [(i, (i + k) % parts) for i in range(parts)])
        for k in range(1, parts)
    ]
    pseudo, certainty = finish(expos, stats, width)
    return pseudo, certainty.reshape(-1)


def solution(mesh):
    return jax.shard_map(
        local,
        mesh=mesh,
        in_specs=(
            P("rows", "cls"),
            P("rows", None, None, None),
            P("rows", None),
            P("rows"),
            P("rows", None, None),
            P("rows"),
            P("rows"),
        ),
        out_specs=(P("rows", "cls"), P("rows")),
        check_vma=False,
    )
```
